128 devices in a mesh: group: 16 (over y_hi, x, core), blk: 8 (over y_lo, z).
Axes of the slice: x: 4, y: 4 (y_hi: 2, y_lo: 2; y = y_hi * 2 + y_lo), z: 4, core: 2. Of those that a mesh axis runs over, the one named last changes fastest.
Arguments:
- embeddings: bfloat16 [131072, 512], P(('group', 'blk')), may hold values from -300 to 300
- cluster: int32 [131072], P(('group', 'blk')), may hold values from 0 to 63, as said below
Outputs:
- max_similarity: float32 [131072], P(('group', 'blk'))
The draws below stay inside these ranges and needn't reach their ends.
Inputs may be any that keep to these rules, and one draw needn't show every extreme that they name: Cluster c belongs to group c // 4, the group of that index along the mesh axis group. Every cluster has 2 or more rows. On the rows of one device, at most 96 belong to clusters of one group, and in every draw some group has exactly 96 rows on every device.
All inputs are finite; a program needn't handle non-finite values.
Results may differ from the reference program's by a relative error of at most 0.00053.
Values may be sent and summed in bfloat16 or wider, within the bound.
No kernel may reach another device: no remote copies, remote signals or barrier semaphores. Data moves between devices by JAX's collectives and lax.ppermute only.
A program may use at most 64 MiB of HBM per device.

```python
import math
import jax
import jax.numpy as jnp
from jax import lax

D = 512
ROWS = 1024
CPG = 4
TOTAL = 131072
CLUSTERS = 64
GROUP_MOST = 12288
N_GROUP = 16
DEVICES = 128


def layout(key):
    keys = jax.random.split(key, 6)
    order = jax.random.permutation(keys[0], N_GROUP).astype(jnp.int32)
    rest = TOTAL - GROUP_MOST
    share = rest // (N_GROUP - 1)
    spare = rest - share * (N_GROUP - 1)
    couples = (N_GROUP - 1) // 2
    moved = jax.random.randint(keys[1], (couples,), 0, share // 3 + 1).astype(jnp.int32)
    ranked = jnp.full((N_GROUP,), share, jnp.int32).at[0].set(GROUP_MOST).at[1].add(spare)
    places_pair = jnp.arange(couples, dtype=jnp.int32)
    ranked = ranked.at[1 + 2 * places_pair].add(-moved).at[2 + 2 * places_pair].add(moved)
    loads = jnp.zeros((N_GROUP,), jnp.int32).at[order].set(ranked)
    weights = jax.random.randint(keys[2], (N_GROUP, CPG), 1, 5).astype(jnp.int32)
    extra = loads - 2 * CPG
    sizes = 2 + extra[:, None] * weights // jnp.sum(weights, axis=1, keepdims=True)
    sizes = sizes.at[:, CPG - 1].set(loads - jnp.sum(sizes[:, :CPG - 1], axis=1))
    sizes = sizes.reshape(CLUSTERS).astype(jnp.int32)
    ends = jnp.cumsum(sizes).astype(jnp.int32)
    starts = ends - sizes
    rows = jnp.arange(TOTAL, dtype=jnp.int32)
    labels = jnp.searchsorted(ends, rows, side='right').astype(jnp.int32)
    device = rows % DEVICES
    local = rows // DEVICES
    shuffle = jax.random.permutation(keys[3], DEVICES).astype(jnp.int32)
    keys_local = jax.random.randint(keys[4], (DEVICES, ROWS), 0, 2 ** 19).astype(jnp.int32) * ROWS + jnp.arange(ROWS, dtype=jnp.int32)[None, :]
    inside = jnp.argsort(keys_local, axis=1).astype(jnp.int32)
    places = shuffle[device] * ROWS + inside[device, local]
    offsets = jax.random.randint(keys[5], (CLUSTERS,), 1, sizes).astype(jnp.int32)
    mine = starts[labels]
    partner = mine + (rows - mine + offsets[labels]) % sizes[labels]
    return (labels, places, partner)


def draw_cluster(key, part):
    labels, places, partner = layout(key)
    return jnp.zeros((TOTAL,), jnp.int32).at[places].set(labels)


def draw_embeddings(key, part):
    labels, places, partner = layout(key)
    key = jax.random.fold_in(key, 7)
    keys = jax.random.split(key, 5)
    centers = jax.random.truncated_normal(keys[0], -4.0, 4.0, (CLUSTERS, D), jnp.float32)
    noise = jax.random.truncated_normal(keys[1], -4.0, 4.0, (TOTAL, D), jnp.float32)
    top = math.log(10.0)
    base = centers[labels] + noise
    jitter = jax.random.truncated_normal(keys[2], -4.0, 4.0, (TOTAL, D), jnp.float32)
    copied = jax.random.uniform(keys[3], (TOTAL,), jnp.float32) < 0.25
    values = jnp.where(copied[:, None], base[partner] + 0.15 * jitter, base)
    scales = jnp.exp(jax.random.uniform(keys[4], (TOTAL,), jnp.float32, 0.0, top))
    values = values * scales[:, None]
    return jnp.zeros((TOTAL, D), jnp.float32).at[places].set(values).astype(jnp.bfloat16)


def setup_inputs(seed: int = 0) -> dict:
    key_of = jax.random.split(jax.random.key(seed), 3)
    return {
        "embeddings": draw_embeddings(jax.random.fold_in(key_of[2], 71), 0),
        "cluster": draw_cluster(jax.random.fold_in(key_of[2], 71), 0),
    }


FLOOR = -4.0

def unit_rows(rows):
    values = rows.astype(jnp.float32)
    scale = lax.rsqrt(lax.optimization_barrier(jnp.mean(values * values, axis=1, keepdims=True)) + 1e-06) / math.sqrt(values.shape[1])
    return (values * scale).astype(jnp.bfloat16)

def reference(embeddings, cluster):
    unit = unit_rows(embeddings).astype(jnp.float32)
    total = unit.shape[0]
    order = jnp.argsort(cluster, stable=True).astype(jnp.int32)
    labels = cluster[order]
    ordered = unit[order]
    first = jnp.searchsorted(labels, labels, side='left').astype(jnp.int32)
    after = jnp.searchsorted(labels, labels, side='right').astype(jnp.int32)
    height = 512
    pieces = total // height
    across = jnp.arange(height, dtype=jnp.int32)

    def one_block(index):
        start = index * height
        rows = lax.dynamic_slice_in_dim(ordered, start, height, 0)
        row_labels = lax.dynamic_slice_in_dim(labels, start, height, 0)
        low = first[start] // height
        high = (after[start + height - 1] - 1) // height + 1

        def add_tile(tile, best):
            other = lax.dynamic_slice_in_dim(ordered, tile * height, height, 0)
            other_labels = lax.dynamic_slice_in_dim(labels, tile * height, height, 0)
            scores = jnp.dot(rows, other.T, precision=lax.Precision.HIGHEST)
            match = (row_labels[:, None] == other_labels[None, :]) & ((start + across)[:, None] != (tile * height + across)[None, :])
            return jnp.maximum(best, lax.optimization_barrier(jnp.max(jnp.where(match, scores, FLOOR), axis=1)))
        return lax.fori_loop(low, high, add_tile, jnp.full((height,), FLOOR, jnp.float32))
    best = lax.map(one_block, jnp.arange(pieces, dtype=jnp.int32)).reshape(total)
    return jnp.zeros((total,), jnp.float32).at[order].set(best)
```

```python
import math

import jax
import jax.numpy as jnp
from jax import lax
from jax.experimental import pallas as pl
from jax.experimental.pallas import tpu as pltpu
from jax.sharding import Mesh, PartitionSpec as P

CPG = 4
GROUPS = 16
SLOTS = 96
WIDTH = GROUPS * SLOTS
ROWS = 1024
D = 512
FLOOR = -4.0

SIZES = {"yh": 2, "x": 4, "c": 2, "yl": 2, "z": 4}
AXES = ("yh", "x", "c", "yl", "z")
PLANE = ("yh", "x", "yl")
RING = ("c", "z")
NT = (((1,), (1,)), ((), ()))
VMEM_LIMIT = 48 * 1024 * 1024

CROSSED = (0, 3)


def to_above():
    return [(c * 4 + z, c * 4 + (z + 1) % 4) for c in range(2) for z in range(4)]


def to_below():
    pairs = []
    for c in range(2):
        for z in range(4):
            lands = (z - 1) % 4
            pairs.append((c * 4 + z, (c ^ 1 if lands in CROSSED else c) * 4 + lands))
    return pairs


def reverse(pairs):
    return [(b, a) for a, b in pairs]


def params():
    return pltpu.CompilerParams(vmem_limit_bytes=VMEM_LIMIT)


def place_kernel(cluster_ref, place_ref, counts_ref):
    step = 256
    kinds = lax.broadcasted_iota(jnp.int32, (128, step), 0)
    before = (
        lax.broadcasted_iota(jnp.int32, (step, step), 0)
        < lax.broadcasted_iota(jnp.int32, (step, step), 1)
    ).astype(jnp.bfloat16)
    total = jnp.zeros((128, 1), jnp.float32)
    row_total = jnp.zeros((8, 128), jnp.float32)
    hots, ranks = [], []
    for first in range(0, ROWS, step):
        hot = kinds == cluster_ref[:, first : first + step]
        hot16 = hot.astype(jnp.bfloat16)
        hots.append(hot)
        ranks.append(jnp.dot(hot16, before, preferred_element_type=jnp.float32) + total)
        total = total + jnp.sum(hot.astype(jnp.float32), axis=1, keepdims=True)
        row_total = row_total + lax.dot_general(
            jnp.ones((8, step), jnp.bfloat16), hot16, NT, preferred_element_type=jnp.float32
        )
    one = lax.broadcasted_iota(jnp.int32, (128, 128), 0)
    other = lax.broadcasted_iota(jnp.int32, (128, 128), 1)
    earlier = ((one // CPG == other // CPG) & (other < one)).astype(jnp.bfloat16)
    base = jnp.dot(
        earlier,
        jnp.broadcast_to(total, (128, 128)).astype(jnp.bfloat16),
        preferred_element_type=jnp.float32,
    )[:, :1]
    base = base + (lax.broadcasted_iota(jnp.int32, (128, 1), 0) // CPG * SLOTS).astype(jnp.float32)
    for k, first in enumerate(range(0, ROWS, step)):
        place = jnp.sum(jnp.where(hots[k], ranks[k] + base, 0.0), axis=0, keepdims=True)
        place_ref[:, first : first + step] = place.astype(jnp.int32)
    counts_ref[...] = row_total[:1].astype(jnp.int32)


def placed(cluster):
    return pl.pallas_call(
        place_kernel,
        out_shape=(
            jax.ShapeDtypeStruct((1, ROWS), jnp.int32),
            jax.ShapeDtypeStruct((1, 128), jnp.int32),
        ),
        compiler_params=params(),
        name="placed",
    )(cluster)


def send_kernel(rows_ref, place_ref, out_ref, unit):
    @pl.when(pl.program_id(0) == 0)
    def _():
        values = rows_ref[...].astype(jnp.float32)
        mean = jnp.mean(values * values, axis=1, keepdims=True)
        scale = lax.rsqrt(mean + 1e-06) / math.sqrt(D)
        unit[...] = (values * scale).astype(jnp.bfloat16)

    height = out_ref.shape[0]
    slot = lax.broadcasted_iota(jnp.int32, (height, ROWS), 0) + pl.program_id(0) * height
    hot = (slot == place_ref[...]).astype(jnp.bfloat16)
    out_ref[...] = jnp.dot(hot, unit[...], preferred_element_type=jnp.float32).astype(jnp.bfloat16)


def send_rows(rows, place):
    height = 256
    return pl.pallas_call(
        send_kernel,
        grid=(WIDTH // height,),
        in_specs=[
            pl.BlockSpec((ROWS, D), lambda i: (0, 0)),
            pl.BlockSpec((1, ROWS), lambda i: (0, 0)),
        ],
        out_specs=pl.BlockSpec((height, D), lambda i: (i, 0)),
        out_shape=jax.ShapeDtypeStruct((WIDTH, D), jnp.bfloat16),
        scratch_shapes=[pltpu.VMEM((ROWS, D), jnp.bfloat16)],
        compiler_params=params(),
        name="send_rows",
    )(rows, place)


def limits(counts_ref, source, core, z, group):
    device = ((source >> 1) * 2 + core) * 8 + (source & 1) * 4 + z
    ends = []
    end = jnp.int32(0)
    for k in range(CPG):
        end = end + counts_ref[device, group * CPG + k]
        ends.append(end)
    return ends


def label_of(slot, ends, empty):
    label = jnp.where(slot < ends[3], 3, empty)
    for k in (2, 1, 0):
        label = jnp.where(slot < ends[k], k, label)
    return label


def row_labels(counts_ref, first_source, sources, core, z, group):
    slot = lax.broadcasted_iota(jnp.int32, (SLOTS, 1), 0)
    return jnp.concatenate(
        [
            label_of(slot, limits(counts_ref, first_source + s, core, z, group), -1)
            for s in range(sources)
        ],
        axis=0,
    )


def column_labels(counts_ref, core, z, group):
    lane = lax.broadcasted_iota(jnp.int32, (1, WIDTH), 1)
    label = jnp.full((1, WIDTH), -2, jnp.int32)
    for s in range(GROUPS):
        ends = limits(counts_ref, jnp.int32(s), core, z, group)
        label = jnp.where(lane >= s * SLOTS, label_of(lane - s * SLOTS, ends, -2), label)
    return label


def lanes_of(best):
    return jnp.max(best.T, axis=0, keepdims=True)


SOURCES = 4
HEIGHT = SOURCES * SLOTS
CHUNK = 512


def own_kernel(where_ref, counts_ref, rows_ref, own_ref, peer_ref, best_ref, labels):
    group, core, z = where_ref[0], where_ref[1], where_ref[2]
    step = pl.program_id(0)

    @pl.when(step == 0)
    def _():
        labels[0:1, :] = column_labels(counts_ref, core, z, group)
        labels[1:2, :] = column_labels(counts_ref, 1 - core, z, group)

    mine = row_labels(counts_ref, step * SOURCES, SOURCES, core, z, group)
    index = lax.broadcasted_iota(jnp.int32, (HEIGHT, 1), 0) + step * HEIGHT
    best = jnp.full((HEIGHT, 128), FLOOR, jnp.float32)
    rows = rows_ref[...]
    for which, ref in enumerate((own_ref, peer_ref)):
        for first in range(0, WIDTH, CHUNK):
            score = lax.dot_general(
                rows, ref[first : first + CHUNK], NT, preferred_element_type=jnp.float32
            )
            match = mine == labels[which : which + 1, first : first + CHUNK]
            if which == 0:
                column = lax.broadcasted_iota(jnp.int32, (1, CHUNK), 1) + first
                match = match & (index != column)
            score = jnp.where(match, score, FLOOR)
            for k in range(0, CHUNK, 128):
                best = jnp.maximum(best, score[:, k : k + 128])
    best_ref[...] = lanes_of(best)


def own_best(where, counts, own, peer):
    return pl.pallas_call(
        own_kernel,
        grid=(WIDTH // HEIGHT,),
        in_specs=[
            pl.BlockSpec(memory_space=pltpu.SMEM),
            pl.BlockSpec(memory_space=pltpu.SMEM),
            pl.BlockSpec((HEIGHT, D), lambda i: (i, 0)),
            pl.BlockSpec((WIDTH, D), lambda i: (0, 0)),
            pl.BlockSpec((WIDTH, D), lambda i: (0, 0)),
        ],
        out_specs=pl.BlockSpec((1, HEIGHT), lambda i: (0, i)),
        out_shape=jax.ShapeDtypeStruct((1, WIDTH), jnp.float32),
        scratch_shapes=[pltpu.VMEM((8, WIDTH), jnp.int32)],
        compiler_params=params(),
        cost_estimate=pl.CostEstimate(
            flops=4 * WIDTH * WIDTH * D, bytes_accessed=6 * WIDTH * D, transcendentals=0
        ),
        name="own_best",
    )(where, counts, own, own, peer)


def far_kernel(
    where_ref, counts_ref, own_ref, peer_ref, below_ref, above_ref, best_ref, above_best_ref, labels, column_best
):
    group, core, z = where_ref[0], where_ref[1], where_ref[2]
    under, over, over_core = where_ref[3], where_ref[4], where_ref[5]
    step = pl.program_id(0)
    tiles = WIDTH // HEIGHT
    kind = step // tiles

    @pl.when(step == 0)
    def _():
        labels[0:1, :] = column_labels(counts_ref, over_core, over, group)
        column_best[...] = jnp.full(column_best.shape, FLOOR, jnp.float32)

    row_core = jnp.where(kind == 1, 1 - core, core)
    row_z = jnp.where(kind == 2, under, z)
    mine = row_labels(counts_ref, (step - kind * tiles) * SOURCES, SOURCES, row_core, row_z, group)

    def visit(rows_ref):
        rows = rows_ref[...]
        best = jnp.full((HEIGHT, 128), FLOOR, jnp.float32)
        for first in range(0, WIDTH, CHUNK):
            score = lax.dot_general(
                rows, above_ref[first : first + CHUNK], NT, preferred_element_type=jnp.float32
            )
            score = jnp.where(mine == labels[0:1, first : first + CHUNK], score, FLOOR)
            for k in range(0, CHUNK, 128):
                best = jnp.maximum(best, score[:, k : k + 128])
            column_best[:, first : first + CHUNK] = jnp.maximum(
                column_best[:, first : first + CHUNK],
                jnp.max(score.reshape(HEIGHT // 8, 8, CHUNK), axis=0),
            )
        best_ref[...] = lanes_of(best)

    pl.when(kind == 0)(lambda: visit(own_ref))
    pl.when(kind == 1)(lambda: visit(peer_ref))
    pl.when(kind == 2)(lambda: visit(below_ref))

    @pl.when(step == 3 * tiles - 1)
    def _():
        above_best_ref[...] = jnp.max(column_best[...], axis=0, keepdims=True)


def far_best(where, counts, own, peer, below, above):
    tiles = WIDTH // HEIGHT

    def block(kind):
        return pl.BlockSpec(
            (HEIGHT, D), lambda i, kind=kind: (jnp.clip(i - kind * tiles, 0, tiles - 1), 0)
        )

    return pl.pallas_call(
        far_kernel,
        grid=(3 * tiles,),
        in_specs=[
            pl.BlockSpec(memory_space=pltpu.SMEM),
            pl.BlockSpec(memory_space=pltpu.SMEM),
            block(0),
            block(1),
            block(2),
            pl.BlockSpec((WIDTH, D), lambda i: (0, 0)),
        ],
        out_specs=(
            pl.BlockSpec((1, HEIGHT), lambda i: (0, i)),
            pl.BlockSpec((1, WIDTH), lambda i: (0, 0)),
        ),
        out_shape=(
            jax.ShapeDtypeStruct((1, 3 * WIDTH), jnp.float32),
            jax.ShapeDtypeStruct((1, WIDTH), jnp.float32),
        ),
        scratch_shapes=[pltpu.VMEM((8, WIDTH), jnp.int32), pltpu.VMEM((8, WIDTH), jnp.float32)],
        compiler_params=params(),
        cost_estimate=pl.CostEstimate(
            flops=6 * WIDTH * WIDTH * D, bytes_accessed=8 * WIDTH * D, transcendentals=0
        ),
        name="far_best",
    )(where, counts, own, peer, below, above)


def join_kernel(*refs):
    best = refs[0][...]
    for ref in refs[1:-1]:
        best = jnp.maximum(best, ref[...])
    out_ref = refs[-1]
    out_ref[...] = jnp.zeros(out_ref.shape, jnp.float32)
    for s in range(GROUPS):
        out_ref[s : s + 1, :SLOTS] = best[:, s * SLOTS : (s + 1) * SLOTS]


def joined(*parts):
    return pl.pallas_call(
        join_kernel,
        out_shape=jax.ShapeDtypeStruct((GROUPS, 128), jnp.float32),
        compiler_params=params(),
        name="joined",
    )(*parts)


def pick_kernel(answers_ref, cluster_ref, place_ref, out_ref):
    group = cluster_ref[...] // CPG
    slot = place_ref[...] - group * SLOTS
    hot = (lax.broadcasted_iota(jnp.int32, (GROUPS, ROWS), 0) == group).astype(jnp.bfloat16)
    rest = answers_ref[...]
    found = jnp.zeros((128, ROWS), jnp.float32)
    for _ in range(3):
        part = rest.astype(jnp.bfloat16)
        rest = rest - part.astype(jnp.float32)
        found = found + lax.dot_general(
            part, hot, (((0,), (0,)), ((), ())), preferred_element_type=jnp.float32
        )
    here = lax.broadcasted_iota(jnp.int32, (128, ROWS), 0) == slot
    out_ref[...] = jnp.sum(jnp.where(here, found, 0.0), axis=0, keepdims=True)


def picked(answers, cluster, place):
    return pl.pallas_call(
        pick_kernel,
        out_shape=jax.ShapeDtypeStruct((1, ROWS), jnp.float32),
        compiler_params=params(),
        name="picked",
    )(answers, cluster, place)


def shards(embeddings, cluster):
    group = lax.axis_index(PLANE)
    core = lax.axis_index("c")
    z = lax.axis_index("z")
    crossed = (z == CROSSED[0]) | (z == CROSSED[1])
    where = jnp.stack(
        [group, core, z, (z + 3) % 4, (z + 1) % 4, jnp.where(crossed, 1 - core, core)]
    ).astype(jnp.int32)
    cluster = cluster.reshape(1, ROWS)
    place, counts = placed(cluster)
    counts = lax.all_gather(counts, AXES, tiled=True)
    sent = send_rows(embeddings, place)
    own = lax.all_to_all(
        sent.reshape(GROUPS, SLOTS, D), PLANE, split_axis=0, concat_axis=0, tiled=True
    ).reshape(WIDTH, D)
    below = lax.ppermute(own, RING, to_above())
    above = lax.ppermute(own, RING, to_below())
    peer = lax.ppermute(own, "c", [(0, 1), (1, 0)])
    best_own = own_best(where, counts, own, peer)
    best, best_above = far_best(where, counts, own, peer, below, above)
    best_far, best_peer, best_below = (best[:, k * WIDTH : (k + 1) * WIDTH] for k in range(3))
    answers = joined(
        best_own,
        best_far,
        lax.ppermute(best_peer, "c", [(0, 1), (1, 0)]),
        lax.ppermute(best_below, RING, reverse(to_above())),
        lax.ppermute(best_above, RING, reverse(to_below())),
    )
    answers = lax.all_to_all(
        answers.reshape(GROUPS, 1, 128), PLANE, split_axis=0, concat_axis=0, tiled=True
    ).reshape(GROUPS, 128)
    return picked(answers, cluster, place).reshape(ROWS)


def solution(mesh):
    devices = mesh.devices.reshape(tuple(SIZES[a] for a in AXES))
    inner = Mesh(devices, AXES)
    return jax.shard_map(
        shards,
        mesh=inner,
        in_specs=(P(AXES, None), P(AXES)),
        out_specs=P(AXES),
        check_vma=False,
    )
```

```python
import math

import jax
import jax.numpy as jnp
from jax import lax
from jax.experimental import pallas as pl
from jax.experimental.pallas import tpu as pltpu
from jax.sharding import Mesh, PartitionSpec as P

CPG = 4
GROUPS = 16
SLOTS = 96
WIDTH = GROUPS * SLOTS
ROWS = 1024
D = 512
FLOOR = -4.0

SIZES = {"yh": 2, "x": 4, "c": 2, "yl": 2, "z": 4}
AXES = ("yh", "x", "c", "yl", "z")
PLANE = ("yh", "x", "yl")
RING = ("c", "z")
NT = (((1,), (1,)), ((), ()))
VMEM_LIMIT = 48 * 1024 * 1024

CROSSED = (0, 3)


def to_above():
    return [(c * 4 + z, c * 4 + (z + 1) % 4) for c in range(2) for z in range(4)]


def to_below():
    pairs = []
    for c in range(2):
        for z in range(4):
            lands = (z - 1) % 4
            pairs.append((c * 4 + z, (c ^ 1 if lands in CROSSED else c) * 4 + lands))
    return pairs


def reverse(pairs):
    return [(b, a) for a, b in pairs]


def params():
    return pltpu.CompilerParams(vmem_limit_bytes=VMEM_LIMIT)


def place_kernel(cluster_ref, place_ref, counts_ref):
    step = 256
    kinds = lax.broadcasted_iota(jnp.int32, (128, step), 0)
    before = (
        lax.broadcasted_iota(jnp.int32, (step, step), 0)
        < lax.broadcasted_iota(jnp.int32, (step, step), 1)
    ).astype(jnp.bfloat16)
    total = jnp.zeros((128, 1), jnp.float32)
    hots, ranks = [], []
    for first in range(0, ROWS, step):
        hot = kinds == cluster_ref[:, first : first + step]
        hot16 = hot.astype(jnp.bfloat16)
        hots.append(hot)
        ranks.append(jnp.dot(hot16, before, preferred_element_type=jnp.float32) + total)
        total = total + jnp.sum(hot.astype(jnp.float32), axis=1, keepdims=True)
    one = lax.broadcasted_iota(jnp.int32, (128, 128), 0)
    other = lax.broadcasted_iota(jnp.int32, (128, 128), 1)
    earlier = ((one // CPG == other // CPG) & (other < one)).astype(jnp.bfloat16)
    base = jnp.dot(
        earlier,
        jnp.broadcast_to(total, (128, 128)).astype(jnp.bfloat16),
        preferred_element_type=jnp.float32,
    )[:, :1]
    base = base + (lax.broadcasted_iota(jnp.int32, (128, 1), 0) // CPG * SLOTS).astype(jnp.float32)
    for k, first in enumerate(range(0, ROWS, step)):
        place = jnp.sum(jnp.where(hots[k], ranks[k] + base, 0.0), axis=0, keepdims=True)
        place_ref[:, first : first + step] = place.astype(jnp.int32)
    group = lax.broadcasted_iota(jnp.int32, (GROUPS, 128), 0)
    kind = lax.broadcasted_iota(jnp.int32, (GROUPS, 128), 1)
    counts = jnp.dot(
        (kind // CPG == group).astype(jnp.bfloat16),
        jnp.where(one % CPG == other, total, 0.0).astype(jnp.bfloat16),
        preferred_element_type=jnp.float32,
    )
    counts_ref[...] = counts.astype(jnp.int32)


def placed(cluster):
    return pl.pallas_call(
        place_kernel,
        out_shape=(
            jax.ShapeDtypeStruct((1, ROWS), jnp.int32),
            jax.ShapeDtypeStruct((GROUPS, 128), jnp.int32),
        ),
        compiler_params=params(),
        name="placed",
    )(cluster)


def send_kernel(rows_ref, place_ref, out_ref, unit):
    @pl.when(pl.program_id(0) == 0)
    def _():
        values = rows_ref[...].astype(jnp.float32)
        mean = jnp.mean(values * values, axis=1, keepdims=True)
        scale = lax.rsqrt(mean + 1e-06) / math.sqrt(D)
        unit[...] = (values * scale).astype(jnp.bfloat16)

    height = out_ref.shape[0]
    slot = lax.broadcasted_iota(jnp.int32, (height, ROWS), 0) + pl.program_id(0) * height
    hot = (slot == place_ref[...]).astype(jnp.bfloat16)
    out_ref[...] = jnp.dot(hot, unit[...], preferred_element_type=jnp.float32).astype(jnp.bfloat16)


def send_rows(rows, place):
    height = 256
    return pl.pallas_call(
        send_kernel,
        grid=(WIDTH // height,),
        in_specs=[
            pl.BlockSpec((ROWS, D), lambda i: (0, 0)),
            pl.BlockSpec((1, ROWS), lambda i: (0, 0)),
        ],
        out_specs=pl.BlockSpec((height, D), lambda i: (i, 0)),
        out_shape=jax.ShapeDtypeStruct((WIDTH, D), jnp.bfloat16),
        scratch_shapes=[pltpu.VMEM((ROWS, D), jnp.bfloat16)],
        compiler_params=params(),
        name="send_rows",
    )(rows, place)


def limits(counts_ref, source):
    ends = []
    end = jnp.int32(0)
    for k in range(CPG):
        end = end + counts_ref[source, k]
        ends.append(end)
    return ends


def label_of(slot, ends, empty):
    label = jnp.where(slot < ends[3], 3, empty)
    for k in (2, 1, 0):
        label = jnp.where(slot < ends[k], k, label)
    return label


def row_labels(counts_ref, first_source, sources):
    slot = lax.broadcasted_iota(jnp.int32, (SLOTS, 1), 0)
    return jnp.concatenate(
        [label_of(slot, limits(counts_ref, first_source + s), -1) for s in range(sources)], axis=0
    )


def column_labels(counts_ref):
    lane = lax.broadcasted_iota(jnp.int32, (1, WIDTH), 1)
    label = jnp.full((1, WIDTH), -2, jnp.int32)
    for s in range(GROUPS):
        ends = limits(counts_ref, s)
        label = jnp.where(lane >= s * SLOTS, label_of(lane - s * SLOTS, ends, -2), label)
    return label


def lanes_of(best):
    return jnp.max(best.T, axis=0, keepdims=True)


SOURCES = 4
HEIGHT = SOURCES * SLOTS
CHUNK = 512


def own_kernel(own_counts, peer_counts, rows_ref, own_ref, peer_ref, best_ref, labels):
    step = pl.program_id(0)

    @pl.when(step == 0)
    def _():
        labels[0:1, :] = column_labels(own_counts)
        labels[1:2, :] = column_labels(peer_counts)

    mine = row_labels(own_counts, step * SOURCES, SOURCES)
    index = lax.broadcasted_iota(jnp.int32, (HEIGHT, 1), 0) + step * HEIGHT
    best = jnp.full((HEIGHT, 128), FLOOR, jnp.float32)
    rows = rows_ref[...]
    for which, ref in enumerate((own_ref, peer_ref)):
        for first in range(0, WIDTH, CHUNK):
            score = lax.dot_general(
                rows, ref[first : first + CHUNK], NT, preferred_element_type=jnp.float32
            )
            match = mine == labels[which : which + 1, first : first + CHUNK]
            if which == 0:
                column = lax.broadcasted_iota(jnp.int32, (1, CHUNK), 1) + first
                match = match & (index != column)
            score = jnp.where(match, score, FLOOR)
            for k in range(0, CHUNK, 128):
                best = jnp.maximum(best, score[:, k : k + 128])
    best_ref[...] = lanes_of(best)


def own_best(own_counts, peer_counts, own, peer):
    return pl.pallas_call(
        own_kernel,
        grid=(WIDTH // HEIGHT,),
        in_specs=[
            pl.BlockSpec(memory_space=pltpu.SMEM),
            pl.BlockSpec(memory_space=pltpu.SMEM),
            pl.BlockSpec((HEIGHT, D), lambda i: (i, 0)),
            pl.BlockSpec((WIDTH, D), lambda i: (0, 0)),
            pl.BlockSpec((WIDTH, D), lambda i: (0, 0)),
        ],
        out_specs=pl.BlockSpec((1, HEIGHT), lambda i: (0, i)),
        out_shape=jax.ShapeDtypeStruct((1, WIDTH), jnp.float32),
        scratch_shapes=[pltpu.VMEM((8, WIDTH), jnp.int32)],
        compiler_params=params(),
        cost_estimate=pl.CostEstimate(
            flops=4 * WIDTH * WIDTH * D, bytes_accessed=6 * WIDTH * D, transcendentals=0
        ),
        name="own_best",
    )(own_counts, peer_counts, own, own, peer)


def far_kernel(
    own_counts,
    peer_counts,
    below_counts,
    above_counts,
    own_ref,
    peer_ref,
    below_ref,
    above_ref,
    best_ref,
    above_best_ref,
    labels,
    column_best,
):
    step = pl.program_id(0)
    tiles = WIDTH // HEIGHT
    kind = step // tiles

    @pl.when(step == 0)
    def _():
        labels[0:1, :] = column_labels(above_counts)
        column_best[...] = jnp.full(column_best.shape, FLOOR, jnp.float32)

    def visit(rows_ref, counts_ref):
        mine = row_labels(counts_ref, (step - kind * tiles) * SOURCES, SOURCES)
        rows = rows_ref[...]
        best = jnp.full((HEIGHT, 128), FLOOR, jnp.float32)
        for first in range(0, WIDTH, CHUNK):
            score = lax.dot_general(
                rows, above_ref[first : first + CHUNK], NT, preferred_element_type=jnp.float32
            )
            score = jnp.where(mine == labels[0:1, first : first + CHUNK], score, FLOOR)
            for k in range(0, CHUNK, 128):
                best = jnp.maximum(best, score[:, k : k + 128])
            column_best[:, first : first + CHUNK] = jnp.maximum(
                column_best[:, first : first + CHUNK],
                jnp.max(score.reshape(HEIGHT // 8, 8, CHUNK), axis=0),
            )
        best_ref[...] = lanes_of(best)

    pl.when(kind == 0)(lambda: visit(own_ref, own_counts))
    pl.when(kind == 1)(lambda: visit(peer_ref, peer_counts))
    pl.when(kind == 2)(lambda: visit(below_ref, below_counts))

    @pl.when(step == 3 * tiles - 1)
    def _():
        above_best_ref[...] = jnp.max(column_best[...], axis=0, keepdims=True)


def far_best(counts, own, peer, below, above):
    tiles = WIDTH // HEIGHT

    def block(kind):
        return pl.BlockSpec(
            (HEIGHT, D), lambda i, kind=kind: (jnp.clip(i - kind * tiles, 0, tiles - 1), 0)
        )

    return pl.pallas_call(
        far_kernel,
        grid=(3 * tiles,),
        in_specs=[
            pl.BlockSpec(memory_space=pltpu.SMEM),
            pl.BlockSpec(memory_space=pltpu.SMEM),
            pl.BlockSpec(memory_space=pltpu.SMEM),
            pl.BlockSpec(memory_space=pltpu.SMEM),
            block(0),
            block(1),
            block(2),
            pl.BlockSpec((WIDTH, D), lambda i: (0, 0)),
        ],
        out_specs=(
            pl.BlockSpec((1, HEIGHT), lambda i: (0, i)),
            pl.BlockSpec((1, WIDTH), lambda i: (0, 0)),
        ),
        out_shape=(
            jax.ShapeDtypeStruct((1, 3 * WIDTH), jnp.float32),
            jax.ShapeDtypeStruct((1, WIDTH), jnp.float32),
        ),
        scratch_shapes=[pltpu.VMEM((8, WIDTH), jnp.int32), pltpu.VMEM((8, WIDTH), jnp.float32)],
        compiler_params=params(),
        cost_estimate=pl.CostEstimate(
            flops=6 * WIDTH * WIDTH * D, bytes_accessed=8 * WIDTH * D, transcendentals=0
        ),
        name="far_best",
    )(*counts, own, peer, below, above)


def join_kernel(*refs):
    best = refs[0][...]
    for ref in refs[1:-1]:
        best = jnp.maximum(best, ref[...])
    out_ref = refs[-1]
    out_ref[...] = jnp.zeros(out_ref.shape, jnp.float32)
    for s in range(GROUPS):
        out_ref[s : s + 1, :SLOTS] = best[:, s * SLOTS : (s + 1) * SLOTS]


def joined(*parts):
    return pl.pallas_call(
        join_kernel,
        out_shape=jax.ShapeDtypeStruct((GROUPS, 128), jnp.float32),
        compiler_params=params(),
        name="joined",
    )(*parts)


def pick_kernel(answers_ref, cluster_ref, place_ref, out_ref):
    group = cluster_ref[...] // CPG
    slot = place_ref[...] - group * SLOTS
    hot = (lax.broadcasted_iota(jnp.int32, (GROUPS, ROWS), 0) == group).astype(jnp.bfloat16)
    rest = answers_ref[...]
    found = jnp.zeros((128, ROWS), jnp.float32)
    for _ in range(3):
        part = rest.astype(jnp.bfloat16)
        rest = rest - part.astype(jnp.float32)
        found = found + lax.dot_general(
            part, hot, (((0,), (0,)), ((), ())), preferred_element_type=jnp.float32
        )
    here = lax.broadcasted_iota(jnp.int32, (128, ROWS), 0) == slot
    out_ref[...] = jnp.sum(jnp.where(here, found, 0.0), axis=0, keepdims=True)


def picked(answers, cluster, place):
    return pl.pallas_call(
        pick_kernel,
        out_shape=jax.ShapeDtypeStruct((1, ROWS), jnp.float32),
        compiler_params=params(),
        name="picked",
    )(answers, cluster, place)


SWAP = [(0, 1), (1, 0)]


def all_to_plane(block):
    return lax.all_to_all(block, PLANE, split_axis=0, concat_axis=0, tiled=True)


def shards(embeddings, cluster):
    cluster = cluster.reshape(1, ROWS)
    place, counts = placed(cluster)
    sent = send_rows(embeddings, place)
    own = all_to_plane(sent.reshape(GROUPS, SLOTS, D)).reshape(WIDTH, D)
    below = lax.ppermute(own, RING, to_above())
    above = lax.ppermute(own, RING, to_below())
    peer = lax.ppermute(own, "c", SWAP)
    counts, own = lax.optimization_barrier((counts, own))
    counts = all_to_plane(counts.reshape(GROUPS, 1, 128)).reshape(GROUPS, 128)
    tables = (
        counts,
        lax.ppermute(counts, "c", SWAP),
        lax.ppermute(counts, RING, to_above()),
        lax.ppermute(counts, RING, to_below()),
    )
    best_own = own_best(tables[0], tables[1], own, peer)
    best, best_above = far_best(tables, own, peer, below, above)
    best_far, best_peer, best_below = (best[:, k * WIDTH : (k + 1) * WIDTH] for k in range(3))
    answers = joined(
        best_own,
        best_far,
        lax.ppermute(best_peer, "c", SWAP),
        lax.ppermute(best_below, RING, reverse(to_above())),
        lax.ppermute(best_above, RING, reverse(to_below())),
    )
    answers = lax.all_to_all(
        answers.reshape(GROUPS, 1, 128), PLANE, split_axis=0, concat_axis=0, tiled=True
    ).reshape(GROUPS, 128)
    return picked(answers, cluster, place).reshape(ROWS)


def solution(mesh):
    devices = mesh.devices.reshape(tuple(SIZES[a] for a in AXES))
    inner = Mesh(devices, AXES)
    return jax.shard_map(
        shards,
        mesh=inner,
        in_specs=(P(AXES, None), P(AXES)),
        out_specs=P(AXES),
        check_vma=False,
    )
```

```python
import math

import jax
import jax.numpy as jnp
from jax import lax
from jax.experimental import pallas as pl
from jax.experimental.pallas import tpu as pltpu
from jax.sharding import Mesh, PartitionSpec as P

CPG = 4
GROUPS = 16
SLOTS = 96
ROWS = 1024
D = 512
LANES = 128
FEATURE_PARTS = D // LANES
PIECES = 3
SHARE = SLOTS // PIECES
PIECE = FEATURE_PARTS * SHARE
TAIL = 16
BLOCK = PIECES * PIECE + TAIL
EARLY = (PIECES - 1) * PIECE
EARLY_BLOCK = PIECE + TAIL
HEIGHT = GROUPS * SHARE
WIDTH = GROUPS * SLOTS
FLOOR = -4.0

SIZES = {"yh": 2, "x": 4, "c": 2, "yl": 2, "z": 4}
AXES = ("yh", "x", "c", "yl", "z")
PLANE = ("yh", "x", "yl")
RING = ("c", "z")
NT = (((1,), (1,)), ((), ()))
VMEM_LIMIT = 48 * 1024 * 1024

CROSSED = (0, 3)


def to_above():
    return [(c * 4 + z, c * 4 + (z + 1) % 4) for c in range(2) for z in range(4)]


def to_below():
    pairs = []
    for c in range(2):
        for z in range(4):
            lands = (z - 1) % 4
            pairs.append((c * 4 + z, (c ^ 1 if lands in CROSSED else c) * 4 + lands))
    return pairs


def reverse(pairs):
    return [(b, a) for a, b in pairs]


def params():
    return pltpu.CompilerParams(vmem_limit_bytes=VMEM_LIMIT)


def place_kernel(cluster_ref, place_ref, ends_ref):
    step = 256
    kinds = lax.broadcasted_iota(jnp.int32, (128, step), 0)
    before = (
        lax.broadcasted_iota(jnp.int32, (step, step), 0)
        < lax.broadcasted_iota(jnp.int32, (step, step), 1)
    ).astype(jnp.bfloat16)
    total = jnp.zeros((128, 1), jnp.float32)
    hots, ranks = [], []
    for first in range(0, ROWS, step):
        hot = kinds == cluster_ref[:, first : first + step]
        hot16 = hot.astype(jnp.bfloat16)
        hots.append(hot)
        ranks.append(jnp.dot(hot16, before, preferred_element_type=jnp.float32) + total)
        total = total + jnp.sum(hot.astype(jnp.float32), axis=1, keepdims=True)
    one = lax.broadcasted_iota(jnp.int32, (128, 128), 0)
    other = lax.broadcasted_iota(jnp.int32, (128, 128), 1)
    earlier = ((one // CPG == other // CPG) & (other < one)).astype(jnp.bfloat16)
    base = jnp.dot(
        earlier,
        jnp.broadcast_to(total, (128, 128)).astype(jnp.bfloat16),
        preferred_element_type=jnp.float32,
    )[:, :1]
    base = base + (lax.broadcasted_iota(jnp.int32, (128, 1), 0) // CPG * SLOTS).astype(jnp.float32)
    for k, first in enumerate(range(0, ROWS, step)):
        place = jnp.sum(jnp.where(hots[k], ranks[k] + base, 0.0), axis=0, keepdims=True)
        place_ref[:, first : first + step] = place.astype(jnp.int32)
    group = lax.broadcasted_iota(jnp.int32, (GROUPS, 128), 0)
    kind = lax.broadcasted_iota(jnp.int32, (GROUPS, 128), 1)
    ends = jnp.dot(
        (kind // CPG == group).astype(jnp.bfloat16),
        jnp.where(one % CPG <= other, total, 0.0).astype(jnp.bfloat16),
        preferred_element_type=jnp.float32,
    )
    ends = jnp.where(kind < CPG, ends, 512.0)
    ends_ref[...] = jnp.broadcast_to(ends[:, None, :], ends_ref.shape).astype(jnp.bfloat16)


def placed(cluster):
    return pl.pallas_call(
        place_kernel,
        out_shape=(
            jax.ShapeDtypeStruct((1, ROWS), jnp.int32),
            jax.ShapeDtypeStruct((GROUPS, TAIL, LANES), jnp.bfloat16),
        ),
        compiler_params=params(),
        name="placed",
    )(cluster)


def send_kernel(rows_ref, place_ref, ends_ref, out_ref, early_ref, unit):
    step = pl.program_id(0)

    @pl.when(step == 0)
    def _():
        values = rows_ref[...].astype(jnp.float32)
        mean = jnp.mean(values * values, axis=1, keepdims=True)
        scale = lax.rsqrt(mean + 1e-06) / math.sqrt(D)
        unit[...] = (values * scale).astype(jnp.bfloat16)

    number = out_ref.shape[0]
    height = number * SLOTS
    slot = lax.broadcasted_iota(jnp.int32, (height, ROWS), 0) + step * height
    hot = (slot == place_ref[...]).astype(jnp.bfloat16)
    rows = jnp.dot(hot, unit[...], preferred_element_type=jnp.float32).astype(jnp.bfloat16)
    rows = rows.reshape(number, SLOTS, D)
    for k in range(PIECES):
        for part in range(FEATURE_PARTS):
            first = k * PIECE + part * SHARE
            out_ref[:, first : first + SHARE] = rows[
                :, k * SHARE : (k + 1) * SHARE, part * LANES : (part + 1) * LANES
            ]
    out_ref[:, PIECES * PIECE :] = ends_ref[...]
    early_ref[...] = out_ref[:, EARLY:]


def send_rows(rows, place, ends):
    number = 4
    return pl.pallas_call(
        send_kernel,
        grid=(GROUPS // number,),
        in_specs=[
            pl.BlockSpec((ROWS, D), lambda i: (0, 0)),
            pl.BlockSpec((1, ROWS), lambda i: (0, 0)),
            pl.BlockSpec((number, TAIL, LANES), lambda i: (i, 0, 0)),
        ],
        out_specs=(
            pl.BlockSpec((number, BLOCK, LANES), lambda i: (i, 0, 0)),
            pl.BlockSpec((number, EARLY_BLOCK, LANES), lambda i: (i, 0, 0)),
        ),
        out_shape=(
            jax.ShapeDtypeStruct((GROUPS, BLOCK, LANES), jnp.bfloat16),
            jax.ShapeDtypeStruct((GROUPS, EARLY_BLOCK, LANES), jnp.bfloat16),
        ),
        scratch_shapes=[pltpu.VMEM((ROWS, D), jnp.bfloat16)],
        compiler_params=params(),
        name="send_rows",
    )(rows, place, ends)


def labels_of(ends, number, empty):
    slot = lax.broadcasted_iota(jnp.int32, (GROUPS, SHARE, LANES), 1) + number * SHARE
    past = jnp.where(slot.astype(jnp.float32) >= ends[:, :1].astype(jnp.float32), 1.0, 0.0)
    label = jnp.sum(past, axis=2, keepdims=True).reshape(HEIGHT, 1)
    return jnp.where(label >= CPG, empty, label)


def row_labels(ends, number):
    return labels_of(ends, number, 5.0)


def column_labels(ends, number):
    label = labels_of(ends, number, 6.0)
    return jnp.broadcast_to(label, (HEIGHT, LANES)).T[:1]


def piece_of(ref, first):
    return jnp.concatenate(
        [
            ref[:, pl.ds(first + part * SHARE, SHARE)].reshape(HEIGHT, LANES)
            for part in range(FEATURE_PARTS)
        ],
        axis=1,
    )


def lanes_of(best):
    return jnp.max(best.T, axis=0, keepdims=True)


def span(number):
    return slice(number * HEIGHT, (number + 1) * HEIGHT)


def scored(rows, mine, columns, labels, numbers, column_best, index=None):
    best = jnp.full((HEIGHT, LANES), FLOOR, jnp.float32)
    for number in numbers:
        score = lax.dot_general(rows, columns[number], NT, preferred_element_type=jnp.float32)
        match = mine == labels[:, span(number)]
        if index is not None:
            column = lax.broadcasted_iota(jnp.int32, (1, HEIGHT), 1) + number * HEIGHT
            match = match & (index != column)
        score = jnp.where(match, score, FLOOR)
        for k in range(0, HEIGHT, LANES):
            best = jnp.maximum(best, score[:, k : k + LANES])
        if column_best is not None:
            column_best[:, span(number)] = jnp.maximum(
                column_best[:, span(number)],
                jnp.max(score.reshape(HEIGHT // 8, 8, HEIGHT), axis=0),
            )
    return best


def own_kernel(own_ref, peer_ref, best_ref, columns, labels):
    own_ends = own_ref[:, PIECES * PIECE :]
    peer_ends = peer_ref[:, PIECES * PIECE :]
    for number in range(PIECES):
        columns[0, number] = piece_of(own_ref, number * PIECE)
        columns[1, number] = piece_of(peer_ref, number * PIECE)
        labels[0:1, span(number)] = column_labels(own_ends, number)
        labels[1:2, span(number)] = column_labels(peer_ends, number)

    def visit(number, _):
        rows = columns[0, number]
        mine = row_labels(own_ends, number)
        index = lax.broadcasted_iota(jnp.int32, (HEIGHT, 1), 0) + number * HEIGHT
        best = jnp.maximum(
            scored(rows, mine, columns.at[0], labels.at[0:1], range(PIECES), None, index),
            scored(rows, mine, columns.at[1], labels.at[1:2], range(PIECES), None),
        )
        best_ref[number] = lanes_of(best)
        return 0

    lax.fori_loop(0, PIECES, visit, 0)


def estimate(pairs):
    return pl.CostEstimate(
        flops=2 * pairs * HEIGHT * HEIGHT * D, bytes_accessed=8 * WIDTH * D, transcendentals=0
    )


BEST = jax.ShapeDtypeStruct((PIECES, 1, HEIGHT), jnp.float32)


def own_best(own, peer):
    return pl.pallas_call(
        own_kernel,
        out_shape=BEST,
        scratch_shapes=[
            pltpu.VMEM((2, PIECES, HEIGHT, D), jnp.bfloat16),
            pltpu.VMEM((8, WIDTH), jnp.float32),
        ],
        compiler_params=params(),
        cost_estimate=estimate(18),
        name="own_best",
    )(own, peer)


def near_kernel(
    own_ref,
    peer_ref,
    below_ref,
    above_ref,
    early_ref,
    old_ref,
    best_ref,
    peer_best_ref,
    below_best_ref,
    above_best_ref,
    columns,
    labels,
    column_best,
):
    above_ends = early_ref[:, EARLY_BLOCK + PIECE :]
    below_ends = early_ref[:, PIECE:EARLY_BLOCK]
    columns[0] = piece_of(above_ref, 0)
    columns[2] = piece_of(early_ref, EARLY_BLOCK)
    for number in (0, 2):
        labels[0:1, span(number)] = column_labels(above_ends, number)
    column_best[...] = jnp.full(column_best.shape, FLOOR, jnp.float32)

    def visit(rows, ends, number):
        mine = row_labels(ends, number)
        return lanes_of(scored(rows, mine, columns, labels.at[0:1], (0, 2), column_best))

    def one(number, _):
        first = pl.multiple_of(number * PIECE, PIECE)
        found = visit(piece_of(own_ref, first), own_ref[:, PIECES * PIECE :], number)
        best_ref[number] = jnp.maximum(found, old_ref[number])
        found = visit(piece_of(peer_ref, first), peer_ref[:, PIECES * PIECE :], number)
        peer_best_ref[number] = found
        return 0

    lax.fori_loop(0, PIECES, one, 0)
    below_best_ref[0] = visit(piece_of(below_ref, 0), below_ends, 0)
    below_best_ref[1] = jnp.full((1, HEIGHT), FLOOR, jnp.float32)
    below_best_ref[2] = visit(piece_of(early_ref, 0), below_ends, 2)
    for number in range(PIECES):
        above_best_ref[number] = jnp.max(column_best[:, span(number)], axis=0, keepdims=True)


def near_best(own, peer, below, above, early, old):
    return pl.pallas_call(
        near_kernel,
        out_shape=(BEST,) * 4,
        scratch_shapes=[
            pltpu.VMEM((PIECES, HEIGHT, D), jnp.bfloat16),
            pltpu.VMEM((8, WIDTH), jnp.float32),
            pltpu.VMEM((8, WIDTH), jnp.float32),
        ],
        compiler_params=params(),
        cost_estimate=estimate(16),
        name="near_best",
    )(own, peer, below, above, early, old)


def last_kernel(
    own_ref,
    peer_ref,
    below_ref,
    above_ref,
    below_late_ref,
    above_late_ref,
    early_ref,
    old_ref,
    old_peer_ref,
    old_below_ref,
    old_above_ref,
    best_ref,
    peer_best_ref,
    below_best_ref,
    above_best_ref,
    columns,
    labels,
    column_best,
):
    above_ends = early_ref[:, EARLY_BLOCK + PIECE :]
    below_ends = early_ref[:, PIECE:EARLY_BLOCK]
    columns[0] = piece_of(above_ref, 0)
    columns[1] = piece_of(above_late_ref, 0)
    columns[2] = piece_of(early_ref, EARLY_BLOCK)
    for number in range(PIECES):
        labels[0:1, span(number)] = column_labels(above_ends, number)
    column_best[...] = jnp.full(column_best.shape, FLOOR, jnp.float32)

    def visit(rows, ends, number, numbers=(1,)):
        mine = row_labels(ends, number)
        return lanes_of(scored(rows, mine, columns, labels.at[0:1], numbers, column_best))

    def one(number, _):
        first = pl.multiple_of(number * PIECE, PIECE)
        found = visit(piece_of(own_ref, first), own_ref[:, PIECES * PIECE :], number)
        best_ref[number] = jnp.maximum(found, old_ref[number])
        found = visit(piece_of(peer_ref, first), peer_ref[:, PIECES * PIECE :], number)
        peer_best_ref[number] = jnp.maximum(found, old_peer_ref[number])
        return 0

    lax.fori_loop(0, PIECES, one, 0)
    found = visit(piece_of(below_ref, 0), below_ends, 0)
    below_best_ref[0] = jnp.maximum(found, old_below_ref[0])
    below_best_ref[1] = visit(piece_of(below_late_ref, 0), below_ends, 1, range(PIECES))
    found = visit(piece_of(early_ref, 0), below_ends, 2)
    below_best_ref[2] = jnp.maximum(found, old_below_ref[2])
    for number in range(PIECES):
        found = jnp.max(column_best[:, span(number)], axis=0, keepdims=True)
        above_best_ref[number] = jnp.maximum(found, old_above_ref[number])


def last_best(*arrays):
    return pl.pallas_call(
        last_kernel,
        out_shape=(BEST,) * 4,
        scratch_shapes=[
            pltpu.VMEM((PIECES, HEIGHT, D), jnp.bfloat16),
            pltpu.VMEM((8, WIDTH), jnp.float32),
            pltpu.VMEM((8, WIDTH), jnp.float32),
        ],
        compiler_params=params(),
        cost_estimate=estimate(11),
        name="last_best",
    )(*arrays)


def join_kernel(*refs):
    best = refs[0][...]
    for ref in refs[1:-1]:
        best = jnp.maximum(best, ref[...])
    out_ref = refs[-1]
    out_ref[...] = jnp.zeros(out_ref.shape, jnp.float32)
    for k in range(PIECES):
        for s in range(GROUPS):
            out_ref[s : s + 1, k * SHARE : (k + 1) * SHARE] = best[k, :, s * SHARE : (s + 1) * SHARE]


def joined(*parts):
    return pl.pallas_call(
        join_kernel,
        out_shape=jax.ShapeDtypeStruct((GROUPS, 128), jnp.float32),
        compiler_params=params(),
        name="joined",
    )(*parts)


def pick_kernel(answers_ref, cluster_ref, place_ref, out_ref):
    group = cluster_ref[...] // CPG
    slot = place_ref[...] - group * SLOTS
    hot = (lax.broadcasted_iota(jnp.int32, (GROUPS, ROWS), 0) == group).astype(jnp.bfloat16)
    rest = answers_ref[...]
    found = jnp.zeros((128, ROWS), jnp.float32)
    for _ in range(3):
        part = rest.astype(jnp.bfloat16)
        rest = rest - part.astype(jnp.float32)
        found = found + lax.dot_general(
            part, hot, (((0,), (0,)), ((), ())), preferred_element_type=jnp.float32
        )
    here = lax.broadcasted_iota(jnp.int32, (128, ROWS), 0) == slot
    out_ref[...] = jnp.sum(jnp.where(here, found, 0.0), axis=0, keepdims=True)


def picked(answers, cluster, place):
    return pl.pallas_call(
        pick_kernel,
        out_shape=jax.ShapeDtypeStruct((1, ROWS), jnp.float32),
        compiler_params=params(),
        name="picked",
    )(answers, cluster, place)


SWAP = [(0, 1), (1, 0)]


def all_to_plane(block):
    return lax.all_to_all(block, PLANE, split_axis=0, concat_axis=0, tiled=True)


def shards(embeddings, cluster):
    cluster = cluster.reshape(1, ROWS)
    place, ends = placed(cluster)
    sent, early = send_rows(embeddings, place, ends)
    early = jnp.concatenate(
        [lax.ppermute(early, RING, to_above()), lax.ppermute(early, RING, to_below())], axis=1
    )
    own = all_to_plane(sent)
    late = [own[:, k * PIECE : (k + 1) * PIECE] for k in range(PIECES - 1)]
    below = [lax.ppermute(block, RING, to_above()) for block in late]
    above = [lax.ppermute(block, RING, to_below()) for block in late]
    early, own = lax.optimization_barrier((early, own))
    peer = lax.ppermute(own, "c", SWAP)
    early = all_to_plane(early)
    best = own_best(own, peer)
    bests = near_best(own, peer, below[0], above[0], early, best)
    best, best_peer, best_below, best_above = last_best(
        own, peer, below[0], above[0], below[1], above[1], early, *bests
    )
    answers = joined(
        best,
        lax.ppermute(best_peer, "c", SWAP),
        lax.ppermute(best_below, RING, reverse(to_above())),
        lax.ppermute(best_above, RING, reverse(to_below())),
    )
    answers = lax.all_to_all(
        answers.reshape(GROUPS, 1, 128), PLANE, split_axis=0, concat_axis=0, tiled=True
    ).reshape(GROUPS, 128)
    return picked(answers, cluster, place).reshape(ROWS)


def solution(mesh):
    devices = mesh.devices.reshape(tuple(SIZES[a] for a in AXES))
    inner = Mesh(devices, AXES)
    return jax.shard_map(
        shards,
        mesh=inner,
        in_specs=(P(AXES, None), P(AXES)),
        out_specs=P(AXES),
        check_vma=False,
    )
```

```python
import math

import jax
import jax.numpy as jnp
from jax import lax
from jax.experimental import pallas as pl
from jax.experimental.pallas import tpu as pltpu
from jax.sharding import Mesh, PartitionSpec as P

CPG = 4
GROUPS = 16
SLOTS = 96
ROWS = 1024
D = 512
LANES = 128
FEATURE_PARTS = D // LANES
PIECES = 3
SHARE = SLOTS // PIECES
PIECE = FEATURE_PARTS * SHARE
TAIL = 16
BLOCK = PIECES * PIECE + TAIL
EARLY = (PIECES - 1) * PIECE
EARLY_BLOCK = PIECE + TAIL
HEIGHT = GROUPS * SHARE
WIDTH = GROUPS * SLOTS
FLOOR = -4.0

SIZES = {"yh": 2, "x": 4, "c": 2, "yl": 2, "z": 4}
AXES = ("yh", "x", "c", "yl", "z")
PLANE = ("yh", "x", "yl")
RING = ("c", "z")
EVERYWHERE = ("z", "c") + PLANE
RING_SIZE = 8
NT = (((1,), (1,)), ((), ()))
VMEM_LIMIT = 32 * 1024 * 1024

CROSSED = (0, 3)


def to_above():
    return [(c * 4 + z, c * 4 + (z + 1) % 4) for c in range(2) for z in range(4)]


def to_below():
    pairs = []
    for c in range(2):
        for z in range(4):
            lands = (z - 1) % 4
            pairs.append((c * 4 + z, (c ^ 1 if lands in CROSSED else c) * 4 + lands))
    return pairs


def params():
    return pltpu.CompilerParams(vmem_limit_bytes=VMEM_LIMIT)


CHUNK = 4


def send_kernel(
    cluster_hbm, rows_hbm, place_ref, early_ref, out_hbm, rows, unit, out, row_sem, out_sems, cluster_ref, cl_sem
):
    cl = pltpu.make_async_copy(cluster_hbm, cluster_ref, cl_sem)
    cl.start()
    fetch = pltpu.make_async_copy(rows_hbm, rows, row_sem)
    fetch.start()
    cl.wait()

    step = 256
    kinds = lax.broadcasted_iota(jnp.int32, (128, step), 0)
    before = (
        lax.broadcasted_iota(jnp.int32, (step, step), 0)
        < lax.broadcasted_iota(jnp.int32, (step, step), 1)
    ).astype(jnp.bfloat16)
    total = jnp.zeros((128, 1), jnp.float32)
    hots, ranks = [], []
    for first in range(0, ROWS, step):
        hot = kinds == cluster_ref[:, first : first + step]
        hots.append(hot)
        rank = jnp.dot(hot.astype(jnp.bfloat16), before, preferred_element_type=jnp.float32)
        ranks.append(rank + total)
        total = total + jnp.sum(hot.astype(jnp.float32), axis=1, keepdims=True)
    one = lax.broadcasted_iota(jnp.int32, (128, 128), 0)
    other = lax.broadcasted_iota(jnp.int32, (128, 128), 1)
    earlier = ((one // CPG == other // CPG) & (other < one)).astype(jnp.bfloat16)
    base = jnp.dot(
        earlier,
        jnp.broadcast_to(total, (128, 128)).astype(jnp.bfloat16),
        preferred_element_type=jnp.float32,
    )[:, :1]
    base = base + (lax.broadcasted_iota(jnp.int32, (128, 1), 0) // CPG * SLOTS).astype(jnp.float32)
    for k, first in enumerate(range(0, ROWS, step)):
        place = jnp.sum(jnp.where(hots[k], ranks[k] + base, 0.0), axis=0, keepdims=True)
        place_ref[:, first : first + step] = place.astype(jnp.int32)

    group = lax.broadcasted_iota(jnp.int32, (GROUPS, 128), 0)
    kind = lax.broadcasted_iota(jnp.int32, (GROUPS, 128), 1)
    ends = jnp.dot(
        (kind // CPG == group).astype(jnp.bfloat16),
        jnp.where(one % CPG <= other, total, 0.0).astype(jnp.bfloat16),
        preferred_element_type=jnp.float32,
    )
    ends = jnp.where(kind < CPG, ends, 512.0)
    ends = jnp.broadcast_to(ends[:, None, :], (GROUPS, TAIL, LANES)).astype(jnp.bfloat16)
    out[:, PIECES * PIECE :] = ends
    early_ref[:, PIECE:] = ends

    fetch.wait()
    values = rows[...].astype(jnp.float32)
    mean = jnp.mean(values * values, axis=1, keepdims=True)
    scale = lax.rsqrt(mean + 1e-06) / math.sqrt(D)
    unit[...] = (values * scale).astype(jnp.bfloat16)

    height = CHUNK * SLOTS
    copies = []
    for chunk in range(GROUPS // CHUNK):
        groups = slice(chunk * CHUNK, (chunk + 1) * CHUNK)
        slot = lax.broadcasted_iota(jnp.int32, (height, ROWS), 0) + chunk * height
        hot = (slot == place_ref[...]).astype(jnp.bfloat16)
        sent = jnp.dot(hot, unit[...], preferred_element_type=jnp.float32).astype(jnp.bfloat16)
        sent = sent.reshape(CHUNK, SLOTS, D)
        for k in range(PIECES):
            for part in range(FEATURE_PARTS):
                first = k * PIECE + part * SHARE
                piece = sent[:, k * SHARE : (k + 1) * SHARE, part * LANES : (part + 1) * LANES]
                out[groups, first : first + SHARE] = piece
                if k == PIECES - 1:
                    early_ref[groups, part * SHARE : (part + 1) * SHARE] = piece
        copy = pltpu.make_async_copy(out.at[groups], out_hbm.at[groups], out_sems.at[chunk])
        copy.start()
        copies.append(copy)
    for copy in copies:
        copy.wait()


VMEM = pl.BlockSpec(memory_space=pltpu.VMEM)
ANY = pl.BlockSpec(memory_space=pltpu.HBM)


def send_rows(cluster, rows):
    return pl.pallas_call(
        send_kernel,
        in_specs=[ANY, ANY],
        out_specs=(VMEM, VMEM, ANY),
        out_shape=(
            jax.ShapeDtypeStruct((1, ROWS), jnp.int32),
            jax.ShapeDtypeStruct((GROUPS, EARLY_BLOCK, LANES), jnp.bfloat16),
            jax.ShapeDtypeStruct((GROUPS, BLOCK, LANES), jnp.bfloat16),
        ),
        scratch_shapes=[
            pltpu.VMEM((ROWS, D), jnp.bfloat16),
            pltpu.VMEM((ROWS, D), jnp.bfloat16),
            pltpu.VMEM((GROUPS, BLOCK, LANES), jnp.bfloat16),
            pltpu.SemaphoreType.DMA,
            pltpu.SemaphoreType.DMA((GROUPS // CHUNK,)),
            pltpu.VMEM((1, ROWS), jnp.int32),
            pltpu.SemaphoreType.DMA,
        ],
        compiler_params=pltpu.CompilerParams(vmem_limit_bytes=63 * 1024 * 1024),
        name="send_rows",
    )(cluster, rows)


def labels_of(ends, number, empty):
    slot = lax.broadcasted_iota(jnp.int32, (GROUPS, SHARE, LANES), 1) + number * SHARE
    past = jnp.where(slot.astype(jnp.float32) >= ends[:, :1].astype(jnp.float32), 1.0, 0.0)
    label = jnp.sum(past, axis=2, keepdims=True).reshape(HEIGHT, 1)
    return jnp.where(label >= CPG, empty, label)


def row_labels(ends, number):
    return labels_of(ends, number, 5.0)


def column_labels(ends, number):
    label = labels_of(ends, number, 6.0)
    return jnp.broadcast_to(label, (HEIGHT, LANES)).T[:1]


def piece_of(ref, first):
    return jnp.concatenate(
        [
            ref[:, pl.ds(first + part * SHARE, SHARE)].reshape(HEIGHT, LANES)
            for part in range(FEATURE_PARTS)
        ],
        axis=1,
    )


def lanes_of(best):
    return jnp.max(best.T, axis=0, keepdims=True)


def span(number):
    return slice(number * HEIGHT, (number + 1) * HEIGHT)


def scored(rows, mine, columns, labels, numbers, column_best, index=None):
    best = jnp.full((HEIGHT, LANES), FLOOR, jnp.float32)
    for number in numbers:
        score = lax.dot_general(rows, columns[number], NT, preferred_element_type=jnp.float32)
        match = mine == labels[:, span(number)]
        if index is not None:
            column = lax.broadcasted_iota(jnp.int32, (1, HEIGHT), 1) + number * HEIGHT
            match = match & (index != column)
        score = jnp.where(match, score, FLOOR)
        for k in range(0, HEIGHT, LANES):
            best = jnp.maximum(best, score[:, k : k + LANES])
        if column_best is not None:
            column_best[:, span(number)] = jnp.maximum(
                column_best[:, span(number)],
                jnp.max(score.reshape(HEIGHT // 8, 8, HEIGHT), axis=0),
            )
    return best


def own_kernel(own_ref, peer_ref, best_ref, columns, labels):
    own_ends = own_ref[:, PIECES * PIECE :]
    peer_ends = peer_ref[:, PIECES * PIECE :]
    for number in range(PIECES):
        columns[0, number] = piece_of(own_ref, number * PIECE)
        columns[1, number] = piece_of(peer_ref, number * PIECE)
        labels[0:1, span(number)] = column_labels(own_ends, number)
        labels[1:2, span(number)] = column_labels(peer_ends, number)

    def visit(number, _):
        rows = columns[0, number]
        mine = row_labels(own_ends, number)
        index = lax.broadcasted_iota(jnp.int32, (HEIGHT, 1), 0) + number * HEIGHT
        best = jnp.maximum(
            scored(rows, mine, columns.at[0], labels.at[0:1], range(PIECES), None, index),
            scored(rows, mine, columns.at[1], labels.at[1:2], range(PIECES), None),
        )
        best_ref[number] = lanes_of(best)
        return 0

    lax.fori_loop(0, PIECES, visit, 0)


def estimate(pairs):
    return pl.CostEstimate(
        flops=2 * pairs * HEIGHT * HEIGHT * D, bytes_accessed=8 * WIDTH * D, transcendentals=0
    )


BEST = jax.ShapeDtypeStruct((PIECES, 1, HEIGHT), jnp.float32)


def own_best(own, peer):
    return pl.pallas_call(
        own_kernel,
        out_shape=BEST,
        scratch_shapes=[
            pltpu.VMEM((2, PIECES, HEIGHT, D), jnp.bfloat16),
            pltpu.VMEM((8, WIDTH), jnp.float32),
        ],
        compiler_params=params(),
        cost_estimate=estimate(18),
        name="own_best",
    )(own, peer)


def near_kernel(
    own_ref,
    peer_ref,
    below_ref,
    above_ref,
    early_ref,
    old_ref,
    best_ref,
    peer_best_ref,
    below_best_ref,
    above_best_ref,
    columns,
    labels,
    column_best,
):
    above_ends = early_ref[:, EARLY_BLOCK + PIECE :]
    below_ends = early_ref[:, PIECE:EARLY_BLOCK]
    columns[0] = piece_of(above_ref, 0)
    columns[2] = piece_of(early_ref, EARLY_BLOCK)
    for number in (0, 2):
        labels[0:1, span(number)] = column_labels(above_ends, number)
    column_best[...] = jnp.full(column_best.shape, FLOOR, jnp.float32)

    def visit(rows, ends, number):
        mine = row_labels(ends, number)
        return lanes_of(scored(rows, mine, columns, labels.at[0:1], (0, 2), column_best))

    def one(number, _):
        first = pl.multiple_of(number * PIECE, PIECE)
        found = visit(piece_of(own_ref, first), own_ref[:, PIECES * PIECE :], number)
        best_ref[number] = jnp.maximum(found, old_ref[number])
        found = visit(piece_of(peer_ref, first), peer_ref[:, PIECES * PIECE :], number)
        peer_best_ref[number] = found
        return 0

    lax.fori_loop(0, PIECES, one, 0)
    below_best_ref[0] = visit(piece_of(below_ref, 0), below_ends, 0)
    below_best_ref[1] = jnp.full((1, HEIGHT), FLOOR, jnp.float32)
    below_best_ref[2] = visit(piece_of(early_ref, 0), below_ends, 2)
    for number in range(PIECES):
        above_best_ref[number] = jnp.max(column_best[:, span(number)], axis=0, keepdims=True)


def near_best(own, peer, below, above, early, old):
    return pl.pallas_call(
        near_kernel,
        out_shape=(BEST,) * 4,
        scratch_shapes=[
            pltpu.VMEM((PIECES, HEIGHT, D), jnp.bfloat16),
            pltpu.VMEM((8, WIDTH), jnp.float32),
            pltpu.VMEM((8, WIDTH), jnp.float32),
        ],
        compiler_params=params(),
        cost_estimate=estimate(16),
        name="near_best",
    )(own, peer, below, above, early, old)


def spread(table, number, row):
    for s in range(GROUPS):
        table[s : s + 1, number * SHARE : (number + 1) * SHARE] = row[:, s * SHARE : (s + 1) * SHARE]


def last_kernel(
    slabs_ref,
    own_ref,
    peer_ref,
    below_ref,
    above_ref,
    below_late_ref,
    above_late_ref,
    early_ref,
    old_ref,
    old_peer_ref,
    old_below_ref,
    old_above_ref,
    out_ref,
    columns,
    labels,
    column_best,
):
    above_ends = early_ref[:, EARLY_BLOCK + PIECE :]
    below_ends = early_ref[:, PIECE:EARLY_BLOCK]
    columns[0] = piece_of(above_ref, 0)
    columns[1] = piece_of(above_late_ref, 0)
    columns[2] = piece_of(early_ref, EARLY_BLOCK)
    for number in range(PIECES):
        labels[0:1, span(number)] = column_labels(above_ends, number)
    column_best[...] = jnp.full(column_best.shape, FLOOR, jnp.float32)

    def visit(rows, ends, number, numbers=(1,)):
        mine = row_labels(ends, number)
        return lanes_of(scored(rows, mine, columns, labels.at[0:1], numbers, column_best))

    out_ref[...] = jnp.full(out_ref.shape, FLOOR, jnp.float32)
    tables = [out_ref.at[slabs_ref[k]] for k in range(4)]
    for number in range(PIECES):
        found = visit(piece_of(own_ref, number * PIECE), own_ref[:, PIECES * PIECE :], number)
        spread(tables[0], number, jnp.maximum(found, old_ref[number]))
    for number in range(PIECES):
        found = visit(piece_of(peer_ref, number * PIECE), peer_ref[:, PIECES * PIECE :], number)
        spread(tables[1], number, jnp.maximum(found, old_peer_ref[number]))
    found = visit(piece_of(below_ref, 0), below_ends, 0)
    spread(tables[2], 0, jnp.maximum(found, old_below_ref[0]))
    found = visit(piece_of(early_ref, 0), below_ends, 2)
    spread(tables[2], 2, jnp.maximum(found, old_below_ref[2]))
    found = visit(piece_of(below_late_ref, 0), below_ends, 1, range(PIECES))
    spread(tables[2], 1, found)
    for number in range(PIECES):
        found = jnp.max(column_best[:, span(number)], axis=0, keepdims=True)
        spread(tables[3], number, jnp.maximum(found, old_above_ref[number]))


def last_best(*arrays):
    return pl.pallas_call(
        last_kernel,
        in_specs=[pl.BlockSpec(memory_space=pltpu.SMEM)] + [VMEM] * 11,
        out_shape=jax.ShapeDtypeStruct((RING_SIZE, GROUPS, LANES), jnp.float32),
        scratch_shapes=[
            pltpu.VMEM((PIECES, HEIGHT, D), jnp.bfloat16),
            pltpu.VMEM((8, WIDTH), jnp.float32),
            pltpu.VMEM((8, WIDTH), jnp.float32),
        ],
        compiler_params=params(),
        cost_estimate=estimate(11),
        name="last_best",
    )(*arrays)


def pick_kernel(answers_ref, cluster_ref, place_ref, out_ref):
    group = cluster_ref[...] // CPG
    slot = place_ref[...] - group * SLOTS
    hot = (lax.broadcasted_iota(jnp.int32, (GROUPS, ROWS), 0) == group).astype(jnp.bfloat16)
    rest = jnp.max(answers_ref[...], axis=0)
    found = jnp.zeros((128, ROWS), jnp.float32)
    for _ in range(3):
        part = rest.astype(jnp.bfloat16)
        rest = rest - part.astype(jnp.float32)
        found = found + lax.dot_general(
            part, hot, (((0,), (0,)), ((), ())), preferred_element_type=jnp.float32
        )
    here = lax.broadcasted_iota(jnp.int32, (128, ROWS), 0) == slot
    out_ref[...] = jnp.sum(jnp.where(here, found, 0.0), axis=0, keepdims=True)


def picked(answers, cluster, place):
    return pl.pallas_call(
        pick_kernel,
        out_shape=jax.ShapeDtypeStruct((1, ROWS), jnp.float32),
        compiler_params=params(),
        name="picked",
    )(answers, cluster, place)


SWAP = [(0, 1), (1, 0)]


def all_to_plane(block):
    return lax.all_to_all(block, PLANE, split_axis=0, concat_axis=0, tiled=True)


def shards(embeddings, cluster):
    cluster = cluster.reshape(1, ROWS)
    place, early, sent = send_rows(cluster, embeddings)
    early = jnp.concatenate(
        [lax.ppermute(early, RING, to_above()), lax.ppermute(early, RING, to_below())], axis=1
    )
    own = all_to_plane(sent)
    late = [own[:, k * PIECE : (k + 1) * PIECE] for k in range(PIECES - 1)]
    below = [lax.ppermute(block, RING, to_above()) for block in late]
    above = [lax.ppermute(block, RING, to_below()) for block in late]
    early, own = lax.optimization_barrier((early, own))
    peer = lax.ppermute(own, "c", SWAP)
    early = all_to_plane(early)
    best = own_best(own, peer)
    bests = near_best(own, peer, below[0], above[0], early, best)
    z = lax.axis_index("z")
    core = lax.axis_index("c")
    crossed = (z == CROSSED[0]) | (z == CROSSED[1])
    slabs = jnp.stack(
        [
            z * 2 + core,
            z * 2 + 1 - core,
            (z + 3) % 4 * 2 + core,
            (z + 1) % 4 * 2 + jnp.where(crossed, 1 - core, core),
        ]
    ).astype(jnp.int32)
    answers = last_best(
        slabs, own, peer, below[0], above[0], below[1], above[1], early, *bests
    )
    answers = lax.all_to_all(
        answers.reshape(RING_SIZE * GROUPS, 1, LANES),
        EVERYWHERE,
        split_axis=0,
        concat_axis=0,
        tiled=True,
    ).reshape(RING_SIZE, GROUPS, LANES)
    return picked(answers, cluster, place).reshape(ROWS)


def solution(mesh):
    devices = mesh.devices.reshape(tuple(SIZES[a] for a in AXES))
    inner = Mesh(devices, AXES)
    return jax.shard_map(
        shards,
        mesh=inner,
        in_specs=(P(AXES, None), P(AXES)),
        out_specs=P(AXES),
        check_vma=False,
    )
```

```python
import math

import jax
import jax.numpy as jnp
from jax import lax
from jax.experimental import pallas as pl
from jax.experimental.pallas import tpu as pltpu
from jax.sharding import Mesh, PartitionSpec as P

CPG = 4
GROUPS = 16
SLOTS = 96
ROWS = 1024
D = 512
LANES = 128
FEATURE_PARTS = D // LANES
PIECES = 3
SHARE = SLOTS // PIECES
PIECE = FEATURE_PARTS * SHARE
TAIL = 16
BLOCK = PIECES * PIECE + TAIL
EARLY = (PIECES - 1) * PIECE
EARLY_BLOCK = PIECE + TAIL
HEIGHT = GROUPS * SHARE
WIDTH = GROUPS * SLOTS
FLOOR = -4.0

SIZES = {"yh": 2, "x": 4, "c": 2, "yl": 2, "z": 4}
AXES = ("yh", "x", "c", "yl", "z")
PLANE = ("yh", "x", "yl")
RING = ("c", "z")
EVERYWHERE = ("z", "c") + PLANE
RING_SIZE = 8
NT = (((1,), (1,)), ((), ()))
VMEM_LIMIT = 32 * 1024 * 1024

CROSSED = (0, 3)


def to_above():
    return [(c * 4 + z, c * 4 + (z + 1) % 4) for c in range(2) for z in range(4)]


def to_below():
    pairs = []
    for c in range(2):
        for z in range(4):
            lands = (z - 1) % 4
            pairs.append((c * 4 + z, (c ^ 1 if lands in CROSSED else c) * 4 + lands))
    return pairs


def params(limit=VMEM_LIMIT):
    return pltpu.CompilerParams(vmem_limit_bytes=limit)


CHUNK = 4


def send_kernel(
    cluster_hbm, rows_hbm, place_ref, early_ref, out_hbm, rows, unit, out, row_sem, out_sems, cluster_ref, cl_sem
):
    cl = pltpu.make_async_copy(cluster_hbm, cluster_ref, cl_sem)
    cl.start()
    fetch = pltpu.make_async_copy(rows_hbm, rows, row_sem)
    fetch.start()
    cl.wait()

    step = 256
    kinds = lax.broadcasted_iota(jnp.int32, (128, step), 0)
    before = (
        lax.broadcasted_iota(jnp.int32, (step, step), 0)
        < lax.broadcasted_iota(jnp.int32, (step, step), 1)
    ).astype(jnp.bfloat16)
    total = jnp.zeros((128, 1), jnp.float32)
    hots, ranks = [], []
    for first in range(0, ROWS, step):
        hot = kinds == cluster_ref[:, first : first + step]
        hots.append(hot)
        rank = jnp.dot(hot.astype(jnp.bfloat16), before, preferred_element_type=jnp.float32)
        ranks.append(rank + total)
        total = total + jnp.sum(hot.astype(jnp.float32), axis=1, keepdims=True)
    one = lax.broadcasted_iota(jnp.int32, (128, 128), 0)
    other = lax.broadcasted_iota(jnp.int32, (128, 128), 1)
    earlier = ((one // CPG == other // CPG) & (other < one)).astype(jnp.bfloat16)
    base = jnp.dot(
        earlier,
        jnp.broadcast_to(total, (128, 128)).astype(jnp.bfloat16),
        preferred_element_type=jnp.float32,
    )[:, :1]
    base = base + (lax.broadcasted_iota(jnp.int32, (128, 1), 0) // CPG * SLOTS).astype(jnp.float32)
    for k, first in enumerate(range(0, ROWS, step)):
        place = jnp.sum(jnp.where(hots[k], ranks[k] + base, 0.0), axis=0, keepdims=True)
        place_ref[:, first : first + step] = place.astype(jnp.int32)

    group = lax.broadcasted_iota(jnp.int32, (GROUPS, 128), 0)
    kind = lax.broadcasted_iota(jnp.int32, (GROUPS, 128), 1)
    ends = jnp.dot(
        (kind // CPG == group).astype(jnp.bfloat16),
        jnp.where(one % CPG <= other, total, 0.0).astype(jnp.bfloat16),
        preferred_element_type=jnp.float32,
    )
    ends = jnp.where(kind < CPG, ends, 512.0)
    ends = jnp.broadcast_to(ends[:, None, :], (GROUPS, TAIL, LANES)).astype(jnp.bfloat16)
    out[:, PIECES * PIECE :] = ends
    early_ref[:, PIECE:] = ends

    fetch.wait()
    values = rows[...].astype(jnp.float32)
    mean = jnp.mean(values * values, axis=1, keepdims=True)
    scale = lax.rsqrt(mean + 1e-06) / math.sqrt(D)
    unit[...] = (values * scale).astype(jnp.bfloat16)

    height = CHUNK * SLOTS
    copies = []
    for chunk in range(GROUPS // CHUNK):
        groups = slice(chunk * CHUNK, (chunk + 1) * CHUNK)
        slot = lax.broadcasted_iota(jnp.int32, (height, ROWS), 0) + chunk * height
        hot = (slot == place_ref[...]).astype(jnp.bfloat16)
        sent = jnp.dot(hot, unit[...], preferred_element_type=jnp.float32).astype(jnp.bfloat16)
        sent = sent.reshape(CHUNK, SLOTS, D)
        for k in range(PIECES):
            for part in range(FEATURE_PARTS):
                first = k * PIECE + part * SHARE
                piece = sent[:, k * SHARE : (k + 1) * SHARE, part * LANES : (part + 1) * LANES]
                out[groups, first : first + SHARE] = piece
                if k == PIECES - 1:
                    early_ref[groups, part * SHARE : (part + 1) * SHARE] = piece
        copy = pltpu.make_async_copy(out.at[groups], out_hbm.at[groups], out_sems.at[chunk])
        copy.start()
        copies.append(copy)
    for copy in copies:
        copy.wait()


VMEM = pl.BlockSpec(memory_space=pltpu.VMEM)
ANY = pl.BlockSpec(memory_space=pltpu.HBM)


def send_rows(cluster, rows):
    return pl.pallas_call(
        send_kernel,
        in_specs=[ANY, ANY],
        out_specs=(VMEM, VMEM, ANY),
        out_shape=(
            jax.ShapeDtypeStruct((1, ROWS), jnp.int32),
            jax.ShapeDtypeStruct((GROUPS, EARLY_BLOCK, LANES), jnp.bfloat16),
            jax.ShapeDtypeStruct((GROUPS, BLOCK, LANES), jnp.bfloat16),
        ),
        scratch_shapes=[
            pltpu.VMEM((ROWS, D), jnp.bfloat16),
            pltpu.VMEM((ROWS, D), jnp.bfloat16),
            pltpu.VMEM((GROUPS, BLOCK, LANES), jnp.bfloat16),
            pltpu.SemaphoreType.DMA,
            pltpu.SemaphoreType.DMA((GROUPS // CHUNK,)),
            pltpu.VMEM((1, ROWS), jnp.int32),
            pltpu.SemaphoreType.DMA,
        ],
        compiler_params=params(63 * 1024 * 1024),
        name="send_rows",
    )(cluster, rows)


def labels_of(ends, number, empty):
    slot = lax.broadcasted_iota(jnp.int32, (GROUPS, SHARE, LANES), 1) + number * SHARE
    past = jnp.where(slot.astype(jnp.float32) >= ends[:, :1].astype(jnp.float32), 1.0, 0.0)
    label = jnp.sum(past, axis=2, keepdims=True).reshape(HEIGHT, 1)
    return jnp.where(label >= CPG, empty, label)


def row_labels(ends, numbers):
    return jnp.concatenate([labels_of(ends, number, 5.0) for number in numbers], axis=0)


def column_labels(ends, number):
    label = labels_of(ends, number, 6.0)
    return jnp.broadcast_to(label, (HEIGHT, LANES)).T[:1]


class Fetch:
    def __init__(self, sems):
        self.sems = sems
        self.number = 0

    def __call__(self, pairs):
        copies = []
        for source, target in pairs:
            copy = pltpu.make_async_copy(source, target, self.sems.at[self.number])
            copy.start()
            copies.append(copy)
            self.number += 1
        return copies

    def piece(self, source, first, target):
        return self(
            (
                source.at[:, pl.ds(first + part * SHARE, SHARE)],
                target.at[:, :, pl.ds(part * LANES, LANES)],
            )
            for part in range(FEATURE_PARTS)
        )

    def block(self, source, target):
        return [c for k in range(PIECES) for c in self.piece(source, k * PIECE, target.at[k])]

    def ends(self, source, first, target):
        return self([(source.at[:, pl.ds(first, TAIL)], target)])


def wait(copies):
    for copy in copies:
        copy.wait()


def span(number):
    return slice(number * HEIGHT, (number + 1) * HEIGHT)


def rows_of(ref):
    return ref[...].reshape(-1, D)


def lanes_of(best):
    found = jnp.max(best.T, axis=0, keepdims=True)
    return [found[:, k : k + HEIGHT] for k in range(0, found.shape[1], HEIGHT)]


def scored(rows, mine, columns, labels, column_best=None, index=None):
    best = jnp.full((rows.shape[0], LANES), FLOOR, jnp.float32)
    for k, piece in enumerate(columns):
        score = lax.dot_general(rows, rows_of(piece), NT, preferred_element_type=jnp.float32)
        match = mine == labels[k]
        if index is not None:
            column = lax.broadcasted_iota(jnp.int32, (1, HEIGHT), 1) + k * HEIGHT
            match = match & (index != column)
        score = jnp.where(match, score, FLOOR)
        for first in range(0, HEIGHT, LANES):
            best = jnp.maximum(best, score[:, first : first + LANES])
        if column_best is not None:
            found = jnp.max(score.reshape(-1, 8, HEIGHT), axis=0)
            column_best[k] = jnp.maximum(column_best[k], found)
    return best


def estimate(pairs):
    return pl.CostEstimate(
        flops=2 * pairs * HEIGHT * HEIGHT * D, bytes_accessed=8 * WIDTH * D, transcendentals=0
    )


def best_shape(pieces=PIECES):
    return jax.ShapeDtypeStruct((pieces, 1, HEIGHT), jnp.float32)


def rows_scratch(pieces):
    return pltpu.VMEM((pieces, GROUPS, SHARE, D), jnp.bfloat16)


def ends_scratch(number):
    return pltpu.VMEM((number, GROUPS, TAIL, LANES), jnp.bfloat16)


def column_scratch(pieces):
    return pltpu.VMEM((pieces, 8, HEIGHT), jnp.float32)


def kernel_call(kernel, name, pairs, in_specs, out_shape, scratch_shapes, copies):
    return pl.pallas_call(
        kernel,
        in_specs=in_specs,
        out_specs=(VMEM,) * len(out_shape),
        out_shape=out_shape,
        scratch_shapes=[*scratch_shapes, pltpu.SemaphoreType.DMA((copies,))],
        compiler_params=params(),
        cost_estimate=estimate(pairs),
        name=name,
    )


def own_kernel(own_hbm, peer_hbm, best_ref, own, peer, ends, sems):
    fetch = Fetch(sems)
    own_ends = fetch.ends(own_hbm, PIECES * PIECE, ends.at[0])
    peer_ends = fetch.ends(peer_hbm, PIECES * PIECE, ends.at[1])
    own_copies = fetch.block(own_hbm, own)
    peer_copies = fetch.block(peer_hbm, peer)
    wait(own_ends)
    wait(peer_ends)
    own_labels = [column_labels(ends[0], k) for k in range(PIECES)]
    peer_labels = [column_labels(ends[1], k) for k in range(PIECES)]
    mine = row_labels(ends[0], range(PIECES))
    index = lax.broadcasted_iota(jnp.int32, (WIDTH, 1), 0)
    wait(own_copies)
    best = scored(rows_of(own), mine, [own.at[k] for k in range(PIECES)], own_labels, None, index)
    wait(peer_copies)
    found = scored(rows_of(own), mine, [peer.at[k] for k in range(PIECES)], peer_labels)
    for k, found in enumerate(lanes_of(jnp.maximum(best, found))):
        best_ref[k] = found


def own_best(own, peer):
    return kernel_call(
        own_kernel,
        "own_best",
        18,
        [ANY, ANY],
        (best_shape(),),
        [rows_scratch(PIECES), rows_scratch(PIECES), ends_scratch(2)],
        2 + 2 * PIECES * FEATURE_PARTS,
    )(own, peer)[0]


def near_kernel(
    own_hbm,
    peer_hbm,
    above_hbm,
    early_hbm,
    old_ref,
    best_ref,
    peer_best_ref,
    below_best_ref,
    above_best_ref,
    rows,
    mine_ref,
    above,
    labels_ref,
    below_mine_ref,
    ends,
    column_best,
    sems,
):
    fetch = Fetch(sems)
    all_ends = fetch.ends(early_hbm, EARLY_BLOCK + PIECE, ends.at[0])
    all_ends += fetch.ends(own_hbm, PIECES * PIECE, ends.at[1])
    all_ends += fetch.ends(peer_hbm, PIECES * PIECE, ends.at[2])
    all_ends += fetch.ends(early_hbm, PIECE, ends.at[3])
    above_copies = fetch.piece(above_hbm, 0, above.at[0])
    above_copies += fetch.piece(early_hbm, EARLY_BLOCK, above.at[1])
    own_copies = fetch.block(own_hbm, rows.at[pl.ds(0, PIECES)])
    peer_copies = fetch.block(peer_hbm, rows.at[pl.ds(PIECES, PIECES)])
    below_copies = fetch.piece(early_hbm, 0, rows.at[2 * PIECES])
    column_best[...] = jnp.full(column_best.shape, FLOOR, jnp.float32)
    wait(all_ends)
    for k in range(PIECES):
        labels_ref[0:1, span(k)] = column_labels(ends[0], k)
    labels = [labels_ref[0:1, span(k)] for k in (0, 2)]
    columns = [above.at[k] for k in range(2)]

    def visit(first, ends, numbers):
        mine = row_labels(ends, numbers)
        mine_ref[first * HEIGHT : (first + len(numbers)) * HEIGHT] = jnp.broadcast_to(
            mine, (len(numbers) * HEIGHT, LANES)
        )
        found = rows_of(rows.at[pl.ds(first, len(numbers))])
        return lanes_of(scored(found, mine, columns, labels, column_best))

    wait(above_copies)
    wait(own_copies)
    for k, found in enumerate(visit(0, ends[1], range(PIECES))):
        best_ref[k] = jnp.maximum(found, old_ref[k])
    wait(peer_copies)
    for k, found in enumerate(visit(PIECES, ends[2], range(PIECES))):
        peer_best_ref[k] = found
    wait(below_copies)
    below_best_ref[0] = visit(2 * PIECES, ends[3], (2,))[0]
    for k in range(2):
        above_best_ref[k] = jnp.max(column_best[k], axis=0, keepdims=True)
    below_mine_ref[...] = jnp.broadcast_to(row_labels(ends[3], range(2)), (2 * HEIGHT, LANES))


def near_best(*arrays):
    return kernel_call(
        near_kernel,
        "near_best",
        14,
        [ANY] * 4 + [VMEM],
        (
            best_shape(),
            best_shape(),
            best_shape(1),
            best_shape(2),
            jax.ShapeDtypeStruct((2 * PIECES + 1, GROUPS, SHARE, D), jnp.bfloat16),
            jax.ShapeDtypeStruct(((2 * PIECES + 1) * HEIGHT, LANES), jnp.float32),
            jax.ShapeDtypeStruct((2, GROUPS, SHARE, D), jnp.bfloat16),
            jax.ShapeDtypeStruct((8, WIDTH), jnp.float32),
            jax.ShapeDtypeStruct((2 * HEIGHT, LANES), jnp.float32),
        ),
        [ends_scratch(4), column_scratch(2)],
        4 + (2 * PIECES + 3) * FEATURE_PARTS,
    )(*arrays)


TABLE = jax.ShapeDtypeStruct((GROUPS, LANES), jnp.float32)


def spread(table, number, row):
    for s in range(GROUPS):
        table[s : s + 1, number * SHARE : (number + 1) * SHARE] = row[:, s * SHARE : (s + 1) * SHARE]


def middle_kernel(
    below_hbm,
    above,
    labels_ref,
    mine_ref,
    old_above_ref,
    below_best_ref,
    above_best_ref,
    below,
    kept_mine_ref,
    column_best,
    sems,
):
    fetch = Fetch(sems)
    copies = fetch.piece(below_hbm, 0, below.at[0])
    copies += fetch.piece(below_hbm, PIECE, below.at[1])
    column_best[...] = jnp.full(column_best.shape, FLOOR, jnp.float32)
    labels = [labels_ref[0:1, span(k)] for k in (0, 2)]
    mine = mine_ref[...]
    kept_mine_ref[...] = mine
    wait(copies)
    columns = [above.at[k] for k in range(2)]
    found = lanes_of(scored(rows_of(below), mine[:, :1], columns, labels, column_best))
    for k in range(2):
        below_best_ref[k] = found[k]
        found_above = jnp.max(column_best[k], axis=0, keepdims=True)
        above_best_ref[k] = jnp.maximum(found_above, old_above_ref[k])


def middle_best(*arrays):
    return kernel_call(
        middle_kernel,
        "middle_best",
        4,
        [ANY] + [VMEM] * 4,
        (
            best_shape(2),
            best_shape(2),
            jax.ShapeDtypeStruct((2, GROUPS, SHARE, D), jnp.bfloat16),
            jax.ShapeDtypeStruct((2 * HEIGHT, LANES), jnp.float32),
        ),
        [column_scratch(2)],
        2 * FEATURE_PARTS,
    )(*arrays)


def last_kernel(
    slabs_ref,
    late_hbm,
    rows,
    mine_ref,
    labels_ref,
    below,
    below_mine_ref,
    old_ref,
    old_peer_ref,
    old_early_ref,
    old_below_ref,
    old_above_ref,
    out_ref,
    late,
    column_best,
    sems,
):
    copies = Fetch(sems).piece(late_hbm, 0, late.at[0])
    column_best[...] = jnp.full(column_best.shape, FLOOR, jnp.float32)
    out_ref[...] = jnp.full(out_ref.shape, FLOOR, jnp.float32)
    labels = [labels_ref[0:1, span(1)]]
    tables = [out_ref.at[slabs_ref[k]] for k in range(4)]
    for k in range(2):
        spread(tables[3], 2 * k, old_above_ref[k])

    def visit(rows, mine):
        return lanes_of(scored(rows_of(rows), mine[:, :1], [late.at[0]], labels, column_best))

    def part(first, number):
        mine = mine_ref[first * HEIGHT : (first + number) * HEIGHT]
        return visit(rows.at[pl.ds(first, number)], mine)

    wait(copies)
    for k, found in enumerate(part(0, PIECES)):
        spread(tables[0], k, jnp.maximum(found, old_ref[k]))
    for k, found in enumerate(part(PIECES, PIECES)):
        spread(tables[1], k, jnp.maximum(found, old_peer_ref[k]))
    spread(tables[2], 2, jnp.maximum(part(2 * PIECES, 1)[0], old_early_ref[0]))
    for k, found in enumerate(visit(below, below_mine_ref[...])):
        spread(tables[2], k, jnp.maximum(found, old_below_ref[k]))
    spread(tables[3], 1, jnp.max(column_best[0], axis=0, keepdims=True))


def last_best(*arrays):
    return kernel_call(
        last_kernel,
        "last_best",
        9,
        [pl.BlockSpec(memory_space=pltpu.SMEM), ANY] + [VMEM] * 10,
        (jax.ShapeDtypeStruct((RING_SIZE, GROUPS, LANES), jnp.float32),),
        [rows_scratch(1), column_scratch(1)],
        FEATURE_PARTS,
    )(*arrays)[0]


def pick_kernel(answers_ref, cluster_ref, place_ref, out_ref):
    group = cluster_ref[...] // CPG
    slot = place_ref[...] - group * SLOTS
    hot = (lax.broadcasted_iota(jnp.int32, (GROUPS, ROWS), 0) == group).astype(jnp.bfloat16)
    rest = jnp.max(answers_ref[...], axis=0)
    found = jnp.zeros((128, ROWS), jnp.float32)
    for _ in range(3):
        part = rest.astype(jnp.bfloat16)
        rest = rest - part.astype(jnp.float32)
        found = found + lax.dot_general(
            part, hot, (((0,), (0,)), ((), ())), preferred_element_type=jnp.float32
        )
    here = lax.broadcasted_iota(jnp.int32, (128, ROWS), 0) == slot
    out_ref[...] = jnp.sum(jnp.where(here, found, 0.0), axis=0, keepdims=True)


def picked(answers, cluster, place):
    return pl.pallas_call(
        pick_kernel,
        out_shape=jax.ShapeDtypeStruct((1, ROWS), jnp.float32),
        compiler_params=params(),
        name="picked",
    )(answers, cluster, place)


SWAP = [(0, 1), (1, 0)]


def all_to_plane(block):
    return lax.all_to_all(block, PLANE, split_axis=0, concat_axis=0, tiled=True)


def shards(embeddings, cluster):
    cluster = cluster.reshape(1, ROWS)
    place, early, sent = send_rows(cluster, embeddings)
    early = jnp.concatenate(
        [lax.ppermute(early, RING, to_above()), lax.ppermute(early, RING, to_below())], axis=1
    )
    own = all_to_plane(sent)
    late = [own[:, k * PIECE : (k + 1) * PIECE] for k in range(PIECES - 1)]
    above = [lax.ppermute(block, RING, to_below()) for block in late]
    below = lax.ppermute(own[:, :EARLY], RING, to_above())
    _, own = lax.optimization_barrier((early, own))
    peer = lax.ppermute(own, "c", SWAP)
    early = all_to_plane(early)
    best = own_best(own, peer)
    best, best_peer, best_early, best_above, rows, mine, columns, labels, below_mine = near_best(
        own, peer, above[0], early, best
    )
    z = lax.axis_index("z")
    core = lax.axis_index("c")
    crossed = (z == CROSSED[0]) | (z == CROSSED[1])
    slabs = jnp.stack(
        [
            z * 2 + core,
            z * 2 + 1 - core,
            (z + 3) % 4 * 2 + core,
            (z + 1) % 4 * 2 + jnp.where(crossed, 1 - core, core),
        ]
    ).astype(jnp.int32)
    best_below, best_above, below, below_mine = middle_best(
        below, columns, labels, below_mine, best_above
    )
    answers = last_best(
        slabs,
        above[1],
        rows,
        mine,
        labels,
        below,
        below_mine,
        best,
        best_peer,
        best_early,
        best_below,
        best_above,
    )
    answers = lax.all_to_all(
        answers.reshape(RING_SIZE * GROUPS, 1, LANES),
        EVERYWHERE,
        split_axis=0,
        concat_axis=0,
        tiled=True,
    ).reshape(RING_SIZE, GROUPS, LANES)
    return picked(answers, cluster, place).reshape(ROWS)


def solution(mesh):
    devices = mesh.devices.reshape(tuple(SIZES[a] for a in AXES))
    inner = Mesh(devices, AXES)
    return jax.shard_map(
        shards,
        mesh=inner,
        in_specs=(P(AXES, None), P(AXES)),
        out_specs=P(AXES),
        check_vma=False,
    )
```

```python
import math

import jax
import jax.numpy as jnp
from jax import lax
from jax.experimental import pallas as pl
from jax.experimental.pallas import tpu as pltpu
from jax.sharding import Mesh, PartitionSpec as P

CPG = 4
GROUPS = 16
SLOTS = 96
ROWS = 1024
D = 512
LANES = 128
FEATURE_PARTS = D // LANES
PIECES = 3
SHARE = SLOTS // PIECES
PIECE = FEATURE_PARTS * SHARE
TAIL = 16
BLOCK = PIECES * PIECE + TAIL
EARLY = (PIECES - 1) * PIECE
EARLY_BLOCK = PIECE + TAIL
HEIGHT = GROUPS * SHARE
WIDTH = GROUPS * SLOTS
FLOOR = -4.0

SIZES = {"yh": 2, "x": 4, "c": 2, "yl": 2, "z": 4}
AXES = ("yh", "x", "c", "yl", "z")
PLANE = ("yh", "x", "yl")
RING = ("c", "z")
EVERYWHERE = ("z", "c") + PLANE
RING_SIZE = 8
NT = (((1,), (1,)), ((), ()))
VMEM_LIMIT = 32 * 1024 * 1024

CROSSED = (0, 3)


def to_above():
    return [(c * 4 + z, c * 4 + (z + 1) % 4) for c in range(2) for z in range(4)]


def to_below():
    pairs = []
    for c in range(2):
        for z in range(4):
            lands = (z - 1) % 4
            pairs.append((c * 4 + z, (c ^ 1 if lands in CROSSED else c) * 4 + lands))
    return pairs


def params(limit=VMEM_LIMIT):
    return pltpu.CompilerParams(vmem_limit_bytes=limit)


CHUNK = 4


def send_kernel(
    cluster_hbm, rows_hbm, place_ref, early_ref, out_hbm, rows, unit, out, row_sem, out_sems, cluster_ref, cl_sem
):
    cl = pltpu.make_async_copy(cluster_hbm, cluster_ref, cl_sem)
    cl.start()
    fetch = pltpu.make_async_copy(rows_hbm, rows, row_sem)
    fetch.start()
    cl.wait()

    step = 256
    kinds = lax.broadcasted_iota(jnp.int32, (128, step), 0)
    before = (
        lax.broadcasted_iota(jnp.int32, (step, step), 0)
        < lax.broadcasted_iota(jnp.int32, (step, step), 1)
    ).astype(jnp.bfloat16)
    total = jnp.zeros((128, 1), jnp.float32)
    hots, ranks = [], []
    for first in range(0, ROWS, step):
        hot = kinds == cluster_ref[:, first : first + step]
        hots.append(hot)
        rank = jnp.dot(hot.astype(jnp.bfloat16), before, preferred_element_type=jnp.float32)
        ranks.append(rank + total)
        total = total + jnp.sum(hot.astype(jnp.float32), axis=1, keepdims=True)
    one = lax.broadcasted_iota(jnp.int32, (128, 128), 0)
    other = lax.broadcasted_iota(jnp.int32, (128, 128), 1)
    earlier = ((one // CPG == other // CPG) & (other < one)).astype(jnp.bfloat16)
    base = jnp.dot(
        earlier,
        jnp.broadcast_to(total, (128, 128)).astype(jnp.bfloat16),
        preferred_element_type=jnp.float32,
    )[:, :1]
    base = base + (lax.broadcasted_iota(jnp.int32, (128, 1), 0) // CPG * SLOTS).astype(jnp.float32)
    for k, first in enumerate(range(0, ROWS, step)):
        place = jnp.sum(jnp.where(hots[k], ranks[k] + base, 0.0), axis=0, keepdims=True)
        place_ref[:, first : first + step] = place.astype(jnp.int32)

    group = lax.broadcasted_iota(jnp.int32, (GROUPS, 128), 0)
    kind = lax.broadcasted_iota(jnp.int32, (GROUPS, 128), 1)
    ends = jnp.dot(
        (kind // CPG == group).astype(jnp.bfloat16),
        jnp.where(one % CPG <= other, total, 0.0).astype(jnp.bfloat16),
        preferred_element_type=jnp.float32,
    )
    ends = jnp.where(kind < CPG, ends, 512.0)
    ends = jnp.broadcast_to(ends[:, None, :], (GROUPS, TAIL, LANES)).astype(jnp.bfloat16)
    out[:, PIECES * PIECE :] = ends
    early_ref[:, PIECE:] = ends

    fetch.wait()
    values = rows[...].astype(jnp.float32)
    mean = jnp.mean(values * values, axis=1, keepdims=True)
    scale = lax.rsqrt(mean + 1e-06) / math.sqrt(D)
    unit[...] = (values * scale).astype(jnp.bfloat16)

    height = CHUNK * SLOTS
    copies = []
    for chunk in range(GROUPS // CHUNK):
        groups = slice(chunk * CHUNK, (chunk + 1) * CHUNK)
        slot = lax.broadcasted_iota(jnp.int32, (height, ROWS), 0) + chunk * height
        hot = (slot == place_ref[...]).astype(jnp.bfloat16)
        sent = jnp.dot(hot, unit[...], preferred_element_type=jnp.float32).astype(jnp.bfloat16)
        sent = sent.reshape(CHUNK, SLOTS, D)
        for k in range(PIECES):
            for part in range(FEATURE_PARTS):
                first = k * PIECE + part * SHARE
                piece = sent[:, k * SHARE : (k + 1) * SHARE, part * LANES : (part + 1) * LANES]
                out[groups, first : first + SHARE] = piece
                if k == PIECES - 1:
                    early_ref[groups, part * SHARE : (part + 1) * SHARE] = piece
        copy = pltpu.make_async_copy(out.at[groups], out_hbm.at[groups], out_sems.at[chunk])
        copy.start()
        copies.append(copy)
    for copy in copies:
        copy.wait()


VMEM = pl.BlockSpec(memory_space=pltpu.VMEM)
ANY = pl.BlockSpec(memory_space=pltpu.HBM)


def send_rows(cluster, rows):
    return pl.pallas_call(
        send_kernel,
        in_specs=[ANY, ANY],
        out_specs=(VMEM, VMEM, ANY),
        out_shape=(
            jax.ShapeDtypeStruct((1, ROWS), jnp.int32),
            jax.ShapeDtypeStruct((GROUPS, EARLY_BLOCK, LANES), jnp.bfloat16),
            jax.ShapeDtypeStruct((GROUPS, BLOCK, LANES), jnp.bfloat16),
        ),
        scratch_shapes=[
            pltpu.VMEM((ROWS, D), jnp.bfloat16),
            pltpu.VMEM((ROWS, D), jnp.bfloat16),
            pltpu.VMEM((GROUPS, BLOCK, LANES), jnp.bfloat16),
            pltpu.SemaphoreType.DMA,
            pltpu.SemaphoreType.DMA((GROUPS // CHUNK,)),
            pltpu.VMEM((1, ROWS), jnp.int32),
            pltpu.SemaphoreType.DMA,
        ],
        compiler_params=params(63 * 1024 * 1024),
        name="send_rows",
    )(cluster, rows)


def labels_of(ends, number, empty):
    slot = lax.broadcasted_iota(jnp.int32, (GROUPS, SHARE, LANES), 1) + number * SHARE
    past = jnp.where(slot.astype(jnp.float32) >= ends[:, :1].astype(jnp.float32), 1.0, 0.0)
    label = jnp.sum(past, axis=2, keepdims=True).reshape(HEIGHT, 1)
    return jnp.where(label >= CPG, empty, label)


def row_labels(ends, numbers):
    return jnp.concatenate([labels_of(ends, number, 5.0) for number in numbers], axis=0)


def column_labels(ends, number):
    label = labels_of(ends, number, 6.0)
    return jnp.broadcast_to(label, (HEIGHT, LANES)).T[:1]


class Fetch:
    def __init__(self, sems):
        self.sems = sems
        self.number = 0

    def __call__(self, pairs):
        copies = []
        for source, target in pairs:
            copy = pltpu.make_async_copy(source, target, self.sems.at[self.number])
            copy.start()
            copies.append(copy)
            self.number += 1
        return copies

    def piece(self, source, first, target):
        return self(
            (
                source.at[:, pl.ds(first + part * SHARE, SHARE)],
                target.at[:, :, pl.ds(part * LANES, LANES)],
            )
            for part in range(FEATURE_PARTS)
        )

    def block(self, source, target):
        return [c for k in range(PIECES) for c in self.piece(source, k * PIECE, target.at[k])]

    def ends(self, source, first, target):
        return self([(source.at[:, pl.ds(first, TAIL)], target)])


def wait(copies):
    for copy in copies:
        copy.wait()


def span(number):
    return slice(number * HEIGHT, (number + 1) * HEIGHT)


def rows_of(ref):
    return ref[...].reshape(-1, D)


def lanes_of(best):
    found = jnp.max(best.T, axis=0, keepdims=True)
    return [found[:, k : k + HEIGHT] for k in range(0, found.shape[1], HEIGHT)]


def scored(rows, mine, columns, labels, column_best=None, index=None):
    best = jnp.full((rows.shape[0], LANES), FLOOR, jnp.float32)
    for k, piece in enumerate(columns):
        score = lax.dot_general(rows, rows_of(piece), NT, preferred_element_type=jnp.float32)
        match = mine == labels[k]
        if index is not None:
            column = lax.broadcasted_iota(jnp.int32, (1, HEIGHT), 1) + k * HEIGHT
            match = match & (index != column)
        score = jnp.where(match, score, FLOOR)
        for first in range(0, HEIGHT, LANES):
            best = jnp.maximum(best, score[:, first : first + LANES])
        if column_best is not None:
            found = jnp.max(score.reshape(-1, 8, HEIGHT), axis=0)
            column_best[k] = jnp.maximum(column_best[k], found)
    return best


def estimate(pairs):
    return pl.CostEstimate(
        flops=2 * pairs * HEIGHT * HEIGHT * D, bytes_accessed=8 * WIDTH * D, transcendentals=0
    )


def best_shape(pieces=PIECES):
    return jax.ShapeDtypeStruct((pieces, 1, HEIGHT), jnp.float32)


def rows_scratch(pieces):
    return pltpu.VMEM((pieces, GROUPS, SHARE, D), jnp.bfloat16)


def ends_scratch(number):
    return pltpu.VMEM((number, GROUPS, TAIL, LANES), jnp.bfloat16)


def column_scratch(pieces):
    return pltpu.VMEM((pieces, 8, HEIGHT), jnp.float32)


def kernel_call(kernel, name, pairs, in_specs, out_shape, scratch_shapes, copies):
    return pl.pallas_call(
        kernel,
        in_specs=in_specs,
        out_specs=(VMEM,) * len(out_shape),
        out_shape=out_shape,
        scratch_shapes=[*scratch_shapes, pltpu.SemaphoreType.DMA((copies,))],
        compiler_params=params(),
        cost_estimate=estimate(pairs),
        name=name,
    )


def own_kernel(own_hbm, peer_hbm, best_ref, own, peer, ends, sems):
    fetch = Fetch(sems)
    own_ends = fetch.ends(own_hbm, PIECES * PIECE, ends.at[0])
    peer_ends = fetch.ends(peer_hbm, PIECES * PIECE, ends.at[1])
    own_copies = fetch.block(own_hbm, own)
    peer_copies = fetch.block(peer_hbm, peer)
    wait(own_ends)
    wait(peer_ends)
    own_labels = [column_labels(ends[0], k) for k in range(PIECES)]
    peer_labels = [column_labels(ends[1], k) for k in range(PIECES)]
    mine = row_labels(ends[0], range(PIECES))
    index = lax.broadcasted_iota(jnp.int32, (WIDTH, 1), 0)
    wait(own_copies)
    best = scored(rows_of(own), mine, [own.at[k] for k in range(PIECES)], own_labels, None, index)
    wait(peer_copies)
    found = scored(rows_of(own), mine, [peer.at[k] for k in range(PIECES)], peer_labels)
    for k, found in enumerate(lanes_of(jnp.maximum(best, found))):
        best_ref[k] = found


def own_best(own, peer):
    return kernel_call(
        own_kernel,
        "own_best",
        18,
        [ANY, ANY],
        (best_shape(),),
        [rows_scratch(PIECES), rows_scratch(PIECES), ends_scratch(2)],
        2 + 2 * PIECES * FEATURE_PARTS,
    )(own, peer)[0]


def near_kernel(
    own_hbm,
    peer_hbm,
    above_hbm,
    early_hbm,
    old_ref,
    best_ref,
    peer_best_ref,
    below_best_ref,
    above_best_ref,
    rows,
    mine_ref,
    above,
    labels_ref,
    below_mine_ref,
    ends,
    column_best,
    sems,
):
    fetch = Fetch(sems)
    all_ends = fetch.ends(early_hbm, 2 * PIECE, ends.at[0])
    all_ends += fetch.ends(own_hbm, PIECES * PIECE, ends.at[1])
    all_ends += fetch.ends(peer_hbm, PIECES * PIECE, ends.at[2])
    above_copies = fetch.piece(above_hbm, 0, above.at[0])
    above_copies += fetch.piece(early_hbm, PIECE, above.at[1])
    own_copies = fetch.block(own_hbm, rows.at[pl.ds(0, PIECES)])
    peer_copies = fetch.block(peer_hbm, rows.at[pl.ds(PIECES, PIECES)])
    below_copies = fetch.piece(early_hbm, 0, rows.at[2 * PIECES])
    column_best[...] = jnp.full(column_best.shape, FLOOR, jnp.float32)
    wait(all_ends)
    above_ends = ends[0].astype(jnp.float32)[:, TAIL // 2 :]
    for k in range(PIECES):
        labels_ref[0:1, span(k)] = column_labels(above_ends, k)
    labels = [labels_ref[0:1, span(k)] for k in (0, 2)]
    columns = [above.at[k] for k in range(2)]

    def visit(first, ends, numbers):
        mine = row_labels(ends, numbers)
        mine_ref[first * HEIGHT : (first + len(numbers)) * HEIGHT] = jnp.broadcast_to(
            mine, (len(numbers) * HEIGHT, LANES)
        )
        found = rows_of(rows.at[pl.ds(first, len(numbers))])
        return lanes_of(scored(found, mine, columns, labels, column_best))

    wait(above_copies)
    wait(own_copies)
    for k, found in enumerate(visit(0, ends[1], range(PIECES))):
        best_ref[k] = jnp.maximum(found, old_ref[k])
    wait(peer_copies)
    for k, found in enumerate(visit(PIECES, ends[2], range(PIECES))):
        peer_best_ref[k] = found
    wait(below_copies)
    below_best_ref[0] = visit(2 * PIECES, ends[0], (2,))[0]
    for k in range(2):
        above_best_ref[k] = jnp.max(column_best[k], axis=0, keepdims=True)
    below_mine_ref[...] = jnp.broadcast_to(row_labels(ends[0], range(2)), (2 * HEIGHT, LANES))


def near_best(*arrays):
    return kernel_call(
        near_kernel,
        "near_best",
        14,
        [ANY] * 4 + [VMEM],
        (
            best_shape(),
            best_shape(),
            best_shape(1),
            best_shape(2),
            jax.ShapeDtypeStruct((2 * PIECES + 1, GROUPS, SHARE, D), jnp.bfloat16),
            jax.ShapeDtypeStruct(((2 * PIECES + 1) * HEIGHT, LANES), jnp.float32),
            jax.ShapeDtypeStruct((2, GROUPS, SHARE, D), jnp.bfloat16),
            jax.ShapeDtypeStruct((8, WIDTH), jnp.float32),
            jax.ShapeDtypeStruct((2 * HEIGHT, LANES), jnp.float32),
        ),
        [ends_scratch(3), column_scratch(2)],
        3 + (2 * PIECES + 3) * FEATURE_PARTS,
    )(*arrays)


TABLE = jax.ShapeDtypeStruct((GROUPS, LANES), jnp.float32)


def spread(table, number, row):
    for s in range(GROUPS):
        table[s : s + 1, number * SHARE : (number + 1) * SHARE] = row[:, s * SHARE : (s + 1) * SHARE]


def middle_kernel(
    below_hbm,
    above,
    labels_ref,
    mine_ref,
    old_above_ref,
    below_best_ref,
    above_best_ref,
    below,
    kept_mine_ref,
    column_best,
    sems,
):
    fetch = Fetch(sems)
    copies = fetch.piece(below_hbm, 0, below.at[0])
    copies += fetch.piece(below_hbm, PIECE, below.at[1])
    column_best[...] = jnp.full(column_best.shape, FLOOR, jnp.float32)
    labels = [labels_ref[0:1, span(k)] for k in (0, 2)]
    mine = mine_ref[...]
    kept_mine_ref[...] = mine
    wait(copies)
    columns = [above.at[k] for k in range(2)]
    found = lanes_of(scored(rows_of(below), mine[:, :1], columns, labels, column_best))
    for k in range(2):
        below_best_ref[k] = found[k]
        found_above = jnp.max(column_best[k], axis=0, keepdims=True)
        above_best_ref[k] = jnp.maximum(found_above, old_above_ref[k])


def middle_best(*arrays):
    return kernel_call(
        middle_kernel,
        "middle_best",
        4,
        [ANY] + [VMEM] * 4,
        (
            best_shape(2),
            best_shape(2),
            jax.ShapeDtypeStruct((2, GROUPS, SHARE, D), jnp.bfloat16),
            jax.ShapeDtypeStruct((2 * HEIGHT, LANES), jnp.float32),
        ),
        [column_scratch(2)],
        2 * FEATURE_PARTS,
    )(*arrays)


def last_kernel(
    slabs_ref,
    late_hbm,
    rows,
    mine_ref,
    labels_ref,
    below,
    below_mine_ref,
    old_ref,
    old_peer_ref,
    old_early_ref,
    old_below_ref,
    old_above_ref,
    out_ref,
    late,
    column_best,
    sems,
):
    copies = Fetch(sems).piece(late_hbm, 0, late.at[0])
    column_best[...] = jnp.full(column_best.shape, FLOOR, jnp.float32)
    out_ref[...] = jnp.full(out_ref.shape, FLOOR, jnp.float32)
    labels = [labels_ref[0:1, span(1)]]
    tables = [out_ref.at[slabs_ref[k]] for k in range(4)]
    for k in range(2):
        spread(tables[3], 2 * k, old_above_ref[k])

    def visit(rows, mine):
        return lanes_of(scored(rows_of(rows), mine[:, :1], [late.at[0]], labels, column_best))

    def part(first, number):
        mine = mine_ref[first * HEIGHT : (first + number) * HEIGHT]
        return visit(rows.at[pl.ds(first, number)], mine)

    wait(copies)
    for k, found in enumerate(part(0, PIECES)):
        spread(tables[0], k, jnp.maximum(found, old_ref[k]))
    for k, found in enumerate(part(PIECES, PIECES)):
        spread(tables[1], k, jnp.maximum(found, old_peer_ref[k]))
    spread(tables[2], 2, jnp.maximum(part(2 * PIECES, 1)[0], old_early_ref[0]))
    for k, found in enumerate(visit(below, below_mine_ref[...])):
        spread(tables[2], k, jnp.maximum(found, old_below_ref[k]))
    spread(tables[3], 1, jnp.max(column_best[0], axis=0, keepdims=True))


def last_best(*arrays):
    return kernel_call(
        last_kernel,
        "last_best",
        9,
        [pl.BlockSpec(memory_space=pltpu.SMEM), ANY] + [VMEM] * 10,
        (jax.ShapeDtypeStruct((RING_SIZE, GROUPS, LANES), jnp.float32),),
        [rows_scratch(1), column_scratch(1)],
        FEATURE_PARTS,
    )(*arrays)[0]


def pick_kernel(answers_ref, cluster_ref, place_ref, out_ref):
    group = cluster_ref[...] // CPG
    slot = place_ref[...] - group * SLOTS
    hot = (lax.broadcasted_iota(jnp.int32, (GROUPS, ROWS), 0) == group).astype(jnp.bfloat16)
    rest = jnp.max(answers_ref[...], axis=0)
    found = jnp.zeros((128, ROWS), jnp.float32)
    for _ in range(3):
        part = rest.astype(jnp.bfloat16)
        rest = rest - part.astype(jnp.float32)
        found = found + lax.dot_general(
            part, hot, (((0,), (0,)), ((), ())), preferred_element_type=jnp.float32
        )
    here = lax.broadcasted_iota(jnp.int32, (128, ROWS), 0) == slot
    out_ref[...] = jnp.sum(jnp.where(here, found, 0.0), axis=0, keepdims=True)


def picked(answers, cluster, place):
    return pl.pallas_call(
        pick_kernel,
        out_shape=jax.ShapeDtypeStruct((1, ROWS), jnp.float32),
        compiler_params=params(),
        name="picked",
    )(answers, cluster, place)


SWAP = [(0, 1), (1, 0)]


def all_to_plane(block):
    return lax.all_to_all(block, PLANE, split_axis=0, concat_axis=0, tiled=True)


def shards(embeddings, cluster):
    cluster = cluster.reshape(1, ROWS)
    place, early, sent = send_rows(cluster, embeddings)
    under = lax.ppermute(early, RING, to_above())
    over = lax.ppermute(early, RING, to_below())
    half = PIECE + TAIL // 2
    early = jnp.concatenate(
        [under[:, :PIECE], over[:, :PIECE], under[:, PIECE:half], over[:, PIECE:half]], axis=1
    )
    own = all_to_plane(sent)
    late = [own[:, k * PIECE : (k + 1) * PIECE] for k in range(PIECES - 1)]
    above = [lax.ppermute(block, RING, to_below()) for block in late]
    below = lax.ppermute(own[:, :EARLY], RING, to_above())
    _, own = lax.optimization_barrier((early, own))
    peer = lax.ppermute(own, "c", SWAP)
    early = all_to_plane(early)
    best = own_best(own, peer)
    best, best_peer, best_early, best_above, rows, mine, columns, labels, below_mine = near_best(
        own, peer, above[0], early, best
    )
    z = lax.axis_index("z")
    core = lax.axis_index("c")
    crossed = (z == CROSSED[0]) | (z == CROSSED[1])
    slabs = jnp.stack(
        [
            z * 2 + core,
            z * 2 + 1 - core,
            (z + 3) % 4 * 2 + core,
            (z + 1) % 4 * 2 + jnp.where(crossed, 1 - core, core),
        ]
    ).astype(jnp.int32)
    best_below, best_above, below, below_mine = middle_best(
        below, columns, labels, below_mine, best_above
    )
    answers = last_best(
        slabs,
        above[1],
        rows,
        mine,
        labels,
        below,
        below_mine,
        best,
        best_peer,
        best_early,
        best_below,
        best_above,
    )
    answers = lax.all_to_all(
        answers.reshape(RING_SIZE * GROUPS, 1, LANES),
        EVERYWHERE,
        split_axis=0,
        concat_axis=0,
        tiled=True,
    ).reshape(RING_SIZE, GROUPS, LANES)
    return picked(answers, cluster, place).reshape(ROWS)


def solution(mesh):
    devices = mesh.devices.reshape(tuple(SIZES[a] for a in AXES))
    inner = Mesh(devices, AXES)
    return jax.shard_map(
        shards,
        mesh=inner,
        in_specs=(P(AXES, None), P(AXES)),
        out_specs=P(AXES),
        check_vma=False,
    )
```

```python
import math

import jax
import jax.numpy as jnp
from jax import lax
from jax.experimental import pallas as pl
from jax.experimental.pallas import tpu as pltpu
from jax.sharding import Mesh, PartitionSpec as P

CPG = 4
GROUPS = 16
SLOTS = 96
ROWS = 1024
D = 512
LANES = 128
FEATURE_PARTS = D // LANES
PIECES = 3
SHARE = SLOTS // PIECES
PIECE = FEATURE_PARTS * SHARE
TAIL = 16
BLOCK = PIECES * PIECE + TAIL
EARLY = (PIECES - 1) * PIECE
EARLY_BLOCK = PIECE + TAIL
HEIGHT = GROUPS * SHARE
WIDTH = GROUPS * SLOTS
FLOOR = -4.0

SIZES = {"yh": 2, "x": 4, "c": 2, "yl": 2, "z": 4}
AXES = ("yh", "x", "c", "yl", "z")
PLANE = ("yh", "x", "yl")
RING = ("c", "z")
EVERYWHERE = ("z", "c") + PLANE
RING_SIZE = 8
NT = (((1,), (1,)), ((), ()))
VMEM_LIMIT = 32 * 1024 * 1024

CROSSED = (0, 3)


def to_above():
    return [(c * 4 + z, c * 4 + (z + 1) % 4) for c in range(2) for z in range(4)]


def to_below():
    pairs = []
    for c in range(2):
        for z in range(4):
            lands = (z - 1) % 4
            pairs.append((c * 4 + z, (c ^ 1 if lands in CROSSED else c) * 4 + lands))
    return pairs


def params(limit=VMEM_LIMIT):
    return pltpu.CompilerParams(vmem_limit_bytes=limit)


CHUNK = 4


def send_kernel(
    cluster_hbm, rows_hbm, place_ref, early_ref, out_hbm, rows, unit, out, row_sem, out_sems, cluster_ref, cl_sem
):
    cl = pltpu.make_async_copy(cluster_hbm, cluster_ref, cl_sem)
    cl.start()
    fetch = pltpu.make_async_copy(rows_hbm, rows, row_sem)
    fetch.start()
    cl.wait()

    step = 256
    kinds = lax.broadcasted_iota(jnp.int32, (128, step), 0)
    before = (
        lax.broadcasted_iota(jnp.int32, (step, step), 0)
        < lax.broadcasted_iota(jnp.int32, (step, step), 1)
    ).astype(jnp.bfloat16)
    total = jnp.zeros((128, 1), jnp.float32)
    hots, ranks = [], []
    for first in range(0, ROWS, step):
        hot = kinds == cluster_ref[:, first : first + step]
        hots.append(hot)
        rank = jnp.dot(hot.astype(jnp.bfloat16), before, preferred_element_type=jnp.float32)
        ranks.append(rank + total)
        total = total + jnp.sum(hot.astype(jnp.float32), axis=1, keepdims=True)
    one = lax.broadcasted_iota(jnp.int32, (128, 128), 0)
    other = lax.broadcasted_iota(jnp.int32, (128, 128), 1)
    earlier = ((one // CPG == other // CPG) & (other < one)).astype(jnp.bfloat16)
    base = jnp.dot(
        earlier,
        jnp.broadcast_to(total, (128, 128)).astype(jnp.bfloat16),
        preferred_element_type=jnp.float32,
    )[:, :1]
    base = base + (lax.broadcasted_iota(jnp.int32, (128, 1), 0) // CPG * SLOTS).astype(jnp.float32)
    for k, first in enumerate(range(0, ROWS, step)):
        place = jnp.sum(jnp.where(hots[k], ranks[k] + base, 0.0), axis=0, keepdims=True)
        place_ref[:, first : first + step] = place.astype(jnp.int32)

    group = lax.broadcasted_iota(jnp.int32, (GROUPS, 128), 0)
    kind = lax.broadcasted_iota(jnp.int32, (GROUPS, 128), 1)
    ends = jnp.dot(
        (kind // CPG == group).astype(jnp.bfloat16),
        jnp.where(one % CPG <= other, total, 0.0).astype(jnp.bfloat16),
        preferred_element_type=jnp.float32,
    )
    ends = jnp.where(kind < CPG, ends, 512.0)
    ends = jnp.broadcast_to(ends[:, None, :], (GROUPS, TAIL, LANES)).astype(jnp.bfloat16)
    out[:, PIECES * PIECE :] = ends
    early_ref[:, PIECE:] = ends

    fetch.wait()
    values = rows[...].astype(jnp.float32)
    mean = jnp.mean(values * values, axis=1, keepdims=True)
    scale = lax.rsqrt(mean + 1e-06) / math.sqrt(D)
    unit[...] = (values * scale).astype(jnp.bfloat16)

    height = CHUNK * SLOTS
    copies = []
    for chunk in range(GROUPS // CHUNK):
        groups = slice(chunk * CHUNK, (chunk + 1) * CHUNK)
        slot = lax.broadcasted_iota(jnp.int32, (height, ROWS), 0) + chunk * height
        hot = (slot == place_ref[...]).astype(jnp.bfloat16)
        sent = jnp.dot(hot, unit[...], preferred_element_type=jnp.float32).astype(jnp.bfloat16)
        sent = sent.reshape(CHUNK, SLOTS, D)
        for k in range(PIECES):
            for part in range(FEATURE_PARTS):
                first = k * PIECE + part * SHARE
                piece = sent[:, k * SHARE : (k + 1) * SHARE, part * LANES : (part + 1) * LANES]
                out[groups, first : first + SHARE] = piece
                if k == PIECES - 1:
                    early_ref[groups, part * SHARE : (part + 1) * SHARE] = piece
        copy = pltpu.make_async_copy(out.at[groups], out_hbm.at[groups], out_sems.at[chunk])
        copy.start()
        copies.append(copy)
    for copy in copies:
        copy.wait()


VMEM = pl.BlockSpec(memory_space=pltpu.VMEM)
ANY = pl.BlockSpec(memory_space=pltpu.HBM)


def send_rows(cluster, rows):
    return pl.pallas_call(
        send_kernel,
        in_specs=[ANY, ANY],
        out_specs=(VMEM, VMEM, ANY),
        out_shape=(
            jax.ShapeDtypeStruct((1, ROWS), jnp.int32),
            jax.ShapeDtypeStruct((GROUPS, EARLY_BLOCK, LANES), jnp.bfloat16),
            jax.ShapeDtypeStruct((GROUPS, BLOCK, LANES), jnp.bfloat16),
        ),
        scratch_shapes=[
            pltpu.VMEM((ROWS, D), jnp.bfloat16),
            pltpu.VMEM((ROWS, D), jnp.bfloat16),
            pltpu.VMEM((GROUPS, BLOCK, LANES), jnp.bfloat16),
            pltpu.SemaphoreType.DMA,
            pltpu.SemaphoreType.DMA((GROUPS // CHUNK,)),
            pltpu.VMEM((1, ROWS), jnp.int32),
            pltpu.SemaphoreType.DMA,
        ],
        compiler_params=params(63 * 1024 * 1024),
        name="send_rows",
    )(cluster, rows)


def labels_of(ends, number, empty):
    slot = lax.broadcasted_iota(jnp.int32, (GROUPS, SHARE, LANES), 1) + number * SHARE
    past = jnp.where(slot.astype(jnp.float32) >= ends[:, :1].astype(jnp.float32), 1.0, 0.0)
    label = jnp.sum(past, axis=2, keepdims=True).reshape(HEIGHT, 1)
    return jnp.where(label >= CPG, empty, label)


def row_labels(ends, numbers):
    return jnp.concatenate([labels_of(ends, number, 5.0) for number in numbers], axis=0)


def column_labels(ends, number):
    label = labels_of(ends, number, 6.0)
    return jnp.broadcast_to(label, (HEIGHT, LANES)).T[:1]


class Fetch:
    def __init__(self, sems):
        self.sems = sems
        self.number = 0

    def __call__(self, pairs):
        copies = []
        for source, target in pairs:
            copy = pltpu.make_async_copy(source, target, self.sems.at[self.number])
            copy.start()
            copies.append(copy)
            self.number += 1
        return copies

    def piece(self, source, first, target):
        return self(
            (
                source.at[:, pl.ds(first + part * SHARE, SHARE)],
                target.at[:, :, pl.ds(part * LANES, LANES)],
            )
            for part in range(FEATURE_PARTS)
        )

    def block(self, source, target):
        return [c for k in range(PIECES) for c in self.piece(source, k * PIECE, target.at[k])]

    def ends(self, source, first, target):
        return self([(source.at[:, pl.ds(first, TAIL)], target)])


def wait(copies):
    for copy in copies:
        copy.wait()


def span(number):
    return slice(number * HEIGHT, (number + 1) * HEIGHT)


def rows_of(ref):
    return ref[...].reshape(-1, D)


def lanes_of(best):
    found = jnp.max(best.T, axis=0, keepdims=True)
    return [found[:, k : k + HEIGHT] for k in range(0, found.shape[1], HEIGHT)]


def scored(rows, mine, columns, labels, column_best=None, index=None):
    best = jnp.full((rows.shape[0], LANES), FLOOR, jnp.float32)
    for k, piece in enumerate(columns):
        score = lax.dot_general(rows, rows_of(piece), NT, preferred_element_type=jnp.float32)
        match = mine == labels[k]
        if index is not None:
            column = lax.broadcasted_iota(jnp.int32, (1, HEIGHT), 1) + k * HEIGHT
            match = match & (index != column)
        score = jnp.where(match, score, FLOOR)
        for first in range(0, HEIGHT, LANES):
            best = jnp.maximum(best, score[:, first : first + LANES])
        if column_best is not None:
            found = jnp.max(score.reshape(-1, 8, HEIGHT), axis=0)
            column_best[k] = jnp.maximum(column_best[k], found)
    return best


def estimate(pairs):
    return pl.CostEstimate(
        flops=2 * pairs * HEIGHT * HEIGHT * D, bytes_accessed=8 * WIDTH * D, transcendentals=0
    )


def best_shape(pieces=PIECES):
    return jax.ShapeDtypeStruct((pieces, 1, HEIGHT), jnp.float32)


def rows_scratch(pieces):
    return pltpu.VMEM((pieces, GROUPS, SHARE, D), jnp.bfloat16)


def ends_scratch(number):
    return pltpu.VMEM((number, GROUPS, TAIL, LANES), jnp.bfloat16)


def column_scratch(pieces):
    return pltpu.VMEM((pieces, 8, HEIGHT), jnp.float32)


def kernel_call(kernel, name, pairs, in_specs, out_shape, scratch_shapes, copies):
    return pl.pallas_call(
        kernel,
        in_specs=in_specs,
        out_specs=(VMEM,) * len(out_shape),
        out_shape=out_shape,
        scratch_shapes=[*scratch_shapes, pltpu.SemaphoreType.DMA((copies,))],
        compiler_params=params(),
        cost_estimate=estimate(pairs),
        name=name,
    )


def own_kernel(own_hbm, peer_hbm, best_ref, own, peer, ends, sems):
    fetch = Fetch(sems)
    own_ends = fetch.ends(own_hbm, PIECES * PIECE, ends.at[0])
    peer_ends = fetch.ends(peer_hbm, PIECES * PIECE, ends.at[1])
    own_copies = fetch.block(own_hbm, own)
    peer_copies = fetch.block(peer_hbm, peer)
    wait(own_ends)
    wait(peer_ends)
    own_labels = [column_labels(ends[0], k) for k in range(PIECES)]
    peer_labels = [column_labels(ends[1], k) for k in range(PIECES)]
    mine = row_labels(ends[0], range(PIECES))
    index = lax.broadcasted_iota(jnp.int32, (WIDTH, 1), 0)
    wait(own_copies)
    best = scored(rows_of(own), mine, [own.at[k] for k in range(PIECES)], own_labels, None, index)
    wait(peer_copies)
    found = scored(rows_of(own), mine, [peer.at[k] for k in range(PIECES)], peer_labels)
    for k, found in enumerate(lanes_of(jnp.maximum(best, found))):
        best_ref[k] = found


def own_best(own, peer):
    return kernel_call(
        own_kernel,
        "own_best",
        18,
        [ANY, ANY],
        (best_shape(),),
        [rows_scratch(PIECES), rows_scratch(PIECES), ends_scratch(2)],
        2 + 2 * PIECES * FEATURE_PARTS,
    )(own, peer)[0]


def near_kernel(
    own_hbm,
    peer_hbm,
    above_hbm,
    early_hbm,
    old_ref,
    best_ref,
    peer_best_ref,
    below_best_ref,
    above_best_ref,
    rows,
    mine_ref,
    above,
    labels_ref,
    below_mine_ref,
    ends,
    column_best,
    sems,
):
    fetch = Fetch(sems)
    all_ends = fetch.ends(early_hbm, 2 * PIECE, ends.at[0])
    all_ends += fetch.ends(own_hbm, PIECES * PIECE, ends.at[1])
    all_ends += fetch.ends(peer_hbm, PIECES * PIECE, ends.at[2])
    above_copies = fetch.piece(above_hbm, 0, above.at[0])
    above_copies += fetch.piece(early_hbm, PIECE, above.at[1])
    own_copies = fetch.block(own_hbm, rows.at[pl.ds(0, PIECES)])
    peer_copies = fetch.block(peer_hbm, rows.at[pl.ds(PIECES, PIECES)])
    below_copies = fetch.piece(early_hbm, 0, rows.at[2 * PIECES])
    column_best[...] = jnp.full(column_best.shape, FLOOR, jnp.float32)
    wait(all_ends)
    above_ends = ends[0].astype(jnp.float32)[:, TAIL // 2 :]
    for k in range(PIECES):
        labels_ref[0:1, span(k)] = column_labels(above_ends, k)
    labels = [labels_ref[0:1, span(k)] for k in (0, 2)]
    columns = [above.at[k] for k in range(2)]

    def visit(first, ends, numbers):
        mine = row_labels(ends, numbers)
        mine_ref[first * HEIGHT : (first + len(numbers)) * HEIGHT] = jnp.broadcast_to(
            mine, (len(numbers) * HEIGHT, LANES)
        )
        found = rows_of(rows.at[pl.ds(first, len(numbers))])
        return lanes_of(scored(found, mine, columns, labels, column_best))

    wait(above_copies)
    wait(own_copies)
    for k, found in enumerate(visit(0, ends[1], range(PIECES))):
        best_ref[k] = jnp.maximum(found, old_ref[k])
    wait(peer_copies)
    for k, found in enumerate(visit(PIECES, ends[2], range(PIECES))):
        peer_best_ref[k] = found
    wait(below_copies)
    below_best_ref[0] = visit(2 * PIECES, ends[0], (2,))[0]
    for k in range(2):
        above_best_ref[k] = jnp.max(column_best[k], axis=0, keepdims=True)
    below_mine_ref[...] = jnp.broadcast_to(row_labels(ends[0], range(2)), (2 * HEIGHT, LANES))


def near_best(*arrays):
    return kernel_call(
        near_kernel,
        "near_best",
        14,
        [ANY] * 4 + [VMEM],
        (
            best_shape(),
            best_shape(),
            best_shape(1),
            best_shape(2),
            jax.ShapeDtypeStruct((2 * PIECES + 1, GROUPS, SHARE, D), jnp.bfloat16),
            jax.ShapeDtypeStruct(((2 * PIECES + 1) * HEIGHT, LANES), jnp.float32),
            jax.ShapeDtypeStruct((2, GROUPS, SHARE, D), jnp.bfloat16),
            jax.ShapeDtypeStruct((8, WIDTH), jnp.float32),
            jax.ShapeDtypeStruct((2 * HEIGHT, LANES), jnp.float32),
        ),
        [ends_scratch(3), column_scratch(2)],
        3 + (2 * PIECES + 3) * FEATURE_PARTS,
    )(*arrays)


TABLE = jax.ShapeDtypeStruct((GROUPS, LANES), jnp.float32)


def spread(table, number, row):
    for s in range(GROUPS):
        table[s : s + 1, number * SHARE : (number + 1) * SHARE] = row[:, s * SHARE : (s + 1) * SHARE]


def middle_kernel(
    below_hbm,
    above,
    labels_ref,
    mine_ref,
    old_above_ref,
    below_best_ref,
    above_best_ref,
    below,
    kept_mine_ref,
    column_best,
    sems,
):
    fetch = Fetch(sems)
    copies = fetch.piece(below_hbm, 0, below.at[0])
    copies += fetch.piece(below_hbm, PIECE, below.at[1])
    column_best[...] = jnp.full(column_best.shape, FLOOR, jnp.float32)
    labels = [labels_ref[0:1, span(k)] for k in (0, 2)]
    mine = mine_ref[...]
    kept_mine_ref[...] = mine
    wait(copies)
    columns = [above.at[k] for k in range(2)]
    found = lanes_of(scored(rows_of(below), mine[:, :1], columns, labels, column_best))
    for k in range(2):
        below_best_ref[k] = found[k]
        found_above = jnp.max(column_best[k], axis=0, keepdims=True)
        above_best_ref[k] = jnp.maximum(found_above, old_above_ref[k])


def middle_best(*arrays):
    return kernel_call(
        middle_kernel,
        "middle_best",
        4,
        [ANY] + [VMEM] * 4,
        (
            best_shape(2),
            best_shape(2),
            jax.ShapeDtypeStruct((2, GROUPS, SHARE, D), jnp.bfloat16),
            jax.ShapeDtypeStruct((2 * HEIGHT, LANES), jnp.float32),
        ),
        [column_scratch(2)],
        2 * FEATURE_PARTS,
    )(*arrays)


def last_kernel(
    slabs_ref,
    late_hbm,
    rows,
    mine_ref,
    labels_ref,
    below,
    below_mine_ref,
    old_ref,
    old_peer_ref,
    old_early_ref,
    old_below_ref,
    old_above_ref,
    out_ref,
    late,
    column_best,
    sems,
):
    copies = Fetch(sems).piece(late_hbm, 0, late.at[0])
    column_best[...] = jnp.full(column_best.shape, FLOOR, jnp.float32)
    out_ref[...] = jnp.full(out_ref.shape, FLOOR, jnp.float32)
    labels = [labels_ref[0:1, span(1)]]
    tables = [out_ref.at[slabs_ref[k]] for k in range(4)]
    for k in range(2):
        spread(tables[3], 2 * k, old_above_ref[k])

    def visit(rows, mine):
        return lanes_of(scored(rows_of(rows), mine[:, :1], [late.at[0]], labels, column_best))

    def part(first, number):
        mine = mine_ref[first * HEIGHT : (first + number) * HEIGHT]
        return visit(rows.at[pl.ds(first, number)], mine)

    wait(copies)
    for k, found in enumerate(part(0, PIECES)):
        spread(tables[0], k, jnp.maximum(found, old_ref[k]))
    for k, found in enumerate(part(PIECES, PIECES)):
        spread(tables[1], k, jnp.maximum(found, old_peer_ref[k]))
    spread(tables[2], 2, jnp.maximum(part(2 * PIECES, 1)[0], old_early_ref[0]))
    for k, found in enumerate(visit(below, below_mine_ref[...])):
        spread(tables[2], k, jnp.maximum(found, old_below_ref[k]))
    spread(tables[3], 1, jnp.max(column_best[0], axis=0, keepdims=True))


def last_best(*arrays):
    return kernel_call(
        last_kernel,
        "last_best",
        9,
        [pl.BlockSpec(memory_space=pltpu.SMEM), ANY] + [VMEM] * 10,
        (jax.ShapeDtypeStruct((RING_SIZE, GROUPS, LANES), jnp.float32),),
        [rows_scratch(1), column_scratch(1)],
        FEATURE_PARTS,
    )(*arrays)[0]


def pick_kernel(answers_ref, cluster_ref, place_ref, out_ref):
    group = cluster_ref[...] // CPG
    slot = place_ref[...] - group * SLOTS
    hot = (lax.broadcasted_iota(jnp.int32, (GROUPS, ROWS), 0) == group).astype(jnp.bfloat16)
    rest = jnp.max(answers_ref[...], axis=0)[:, :SLOTS]
    found = jnp.zeros((SLOTS, ROWS), jnp.float32)
    for _ in range(3):
        part = rest.astype(jnp.bfloat16)
        rest = rest - part.astype(jnp.float32)
        found = found + lax.dot_general(
            part, hot, (((0,), (0,)), ((), ())), preferred_element_type=jnp.float32
        )
    here = lax.broadcasted_iota(jnp.int32, (SLOTS, ROWS), 0) == slot
    out_ref[...] = jnp.sum(jnp.where(here, found, 0.0), axis=0, keepdims=True)


def picked(answers, cluster, place):
    return pl.pallas_call(
        pick_kernel,
        out_shape=jax.ShapeDtypeStruct((1, ROWS), jnp.float32),
        compiler_params=params(),
        name="picked",
    )(answers, cluster, place)


SWAP = [(0, 1), (1, 0)]


def all_to_plane(block):
    return lax.all_to_all(block, PLANE, split_axis=0, concat_axis=0, tiled=True)


def shards(embeddings, cluster):
    cluster = cluster.reshape(1, ROWS)
    place, early, sent = send_rows(cluster, embeddings)
    under = lax.ppermute(early, RING, to_above())
    over = lax.ppermute(early, RING, to_below())
    half = PIECE + TAIL // 2
    early = jnp.concatenate(
        [under[:, :PIECE], over[:, :PIECE], under[:, PIECE:half], over[:, PIECE:half]], axis=1
    )
    own = all_to_plane(sent)
    late = [own[:, k * PIECE : (k + 1) * PIECE] for k in range(PIECES - 1)]
    above = [lax.ppermute(block, RING, to_below()) for block in late]
    below = lax.ppermute(own[:, :EARLY], RING, to_above())
    _, own = lax.optimization_barrier((early, own))
    peer = lax.ppermute(own, "c", SWAP)
    early = all_to_plane(early)
    best = own_best(own, peer)
    best, best_peer, best_early, best_above, rows, mine, columns, labels, below_mine = near_best(
        own, peer, above[0], early, best
    )
    z = lax.axis_index("z")
    core = lax.axis_index("c")
    crossed = (z == CROSSED[0]) | (z == CROSSED[1])
    slabs = jnp.stack(
        [
            z * 2 + core,
            z * 2 + 1 - core,
            (z + 3) % 4 * 2 + core,
            (z + 1) % 4 * 2 + jnp.where(crossed, 1 - core, core),
        ]
    ).astype(jnp.int32)
    best_below, best_above, below, below_mine = middle_best(
        below, columns, labels, below_mine, best_above
    )
    answers = last_best(
        slabs,
        above[1],
        rows,
        mine,
        labels,
        below,
        below_mine,
        best,
        best_peer,
        best_early,
        best_below,
        best_above,
    )
    answers = lax.all_to_all(
        answers.reshape(RING_SIZE * GROUPS, 1, LANES),
        EVERYWHERE,
        split_axis=0,
        concat_axis=0,
        tiled=True,
    ).reshape(RING_SIZE, GROUPS, LANES)
    return picked(answers, cluster, place).reshape(ROWS)


def solution(mesh):
    devices = mesh.devices.reshape(tuple(SIZES[a] for a in AXES))
    inner = Mesh(devices, AXES)
    return jax.shard_map(
        shards,
        mesh=inner,
        in_specs=(P(AXES, None), P(AXES)),
        out_specs=P(AXES),
        check_vma=False,
    )
```
